32 devices in a mesh: rec: 4 (over z), tm: 8 (over y, x, core).
Axes of the slice: x: 2, y: 2, z: 4, core: 2. Of those that a mesh axis runs over, the one named last changes fastest.
Arguments:
- audio: float32 [4, 40960], P('rec', 'tm'), may hold values from -100 to 100, as said below
- conv0_weight: float32 [10, 512], replicated, may hold values from -2 to 2
- norm_gain: float32 [512], replicated, may hold values from 0.25 to 1.75
- norm_bias: float32 [512], replicated, may hold values from -3 to 3
- conv1_weight: bfloat16 [1536, 512], replicated, may hold values from -0.25 to 0.25
- conv2_weight: bfloat16 [1536, 512], replicated, may hold values from -0.25 to 0.25
- cotangent: bfloat16 [4, 2048, 512], P('rec', 'tm'), may hold values from -0.09375 to 0.09375
Outputs:
- features: bfloat16 [4, 2048, 512], P('rec', 'tm')
- grad_conv0: float32 [10, 512], replicated
- grad_gain: float32 [512], replicated
- grad_bias: float32 [512], replicated
- grad_conv1: float32 [1536, 512], replicated
- grad_conv2: float32 [1536, 512], replicated
The draws below stay inside these ranges and needn't reach their ends.
Inputs may be any that keep to these rules, and one draw needn't show every extreme that they name: `audio`: recorded waveforms, one row a recording.
All inputs are finite; a program needn't handle non-finite values.
Results may differ from the reference program's by a relative error of at most 0.0095.
Values may be sent and summed in bfloat16 or wider, within the bound.
A program may use at most 64 MiB of HBM per device.

```python
import math
import jax
import jax.numpy as jnp
from jax import lax

C = 512
FRAMES_DEV = 256
RECS = 4
FRAMES = 2048
SAMPLES = 40960


def draw_audio(key, part):
    noise_key = jax.random.fold_in(key, 11)
    level_key = jax.random.fold_in(key, 23)
    piece_key = jax.random.fold_in(key, 37)
    span = 20 * FRAMES_DEV
    pieces = SAMPLES // span
    position = jnp.arange(SAMPLES, dtype=jnp.float32) / (SAMPLES * 1.0)
    level = jnp.exp(jax.random.uniform(level_key, (RECS, 1), jnp.float32, math.log(0.5), math.log(2.0)))
    piece_level = jnp.exp(jax.random.uniform(piece_key, (RECS, pieces, 1), jnp.float32, math.log(0.25), math.log(4.0)))
    rough = jnp.broadcast_to(piece_level, (RECS, pieces, span)).reshape(RECS, SAMPLES)
    noise = jnp.clip(jax.random.normal(noise_key, (RECS, SAMPLES), jnp.float32), -4.0, 4.0)
    envelope = 3.0 * jnp.exp(position * -math.log(3.0))
    return jnp.clip(noise * envelope[None, :] * level * rough, -100.0, 100.0)


def strengthened(values, key, source, target, shards_of, factor):
    def block_of(dim):
        return (jnp.arange(values.shape[dim]) // (values.shape[dim] // shards_of)).reshape((-1,) + (1,) * (values.ndim - 1 - dim))

    first = jax.random.permutation(key, shards_of)[block_of(target)]
    other_side = (block_of(target) + shards_of // 2) % shards_of
    return jnp.where((block_of(source) == first) | (block_of(source) == other_side), factor * values, values)


def levels(own_key, dims, shards, least, high):
    loudness, own = 1.0, jax.random.fold_in(own_key, 6)
    for dim, shards_of in shards:
        steps = jnp.exp(jax.random.uniform(jax.random.fold_in(own, dim), (shards_of,), jnp.float32, least / len(shards), high / len(shards)))
        loudness = loudness * jnp.repeat(steps, dims[dim] // shards_of).reshape([-1 if axis == dim else 1 for axis in range(len(dims))])
    return loudness


def bell_draw(rng, dims, width, bound, shards=(), kind=jnp.bfloat16):
    drawn = jax.random.normal(rng, dims, jnp.float32) * width
    if len(shards) > 0:
        drawn = levels(rng, dims, shards, -0.22, 0.18) * drawn
    return jnp.clip(drawn, min=-bound, max=bound).astype(kind)


def gaussian_with(own_key, dims, spread, limit, split, heavy, held_as=jnp.bfloat16):
    drawn = spread * jax.random.normal(own_key, dims, jnp.float32)
    if split:
        drawn = drawn * levels(own_key, dims, split, -0.22, 0.18)
    return jnp.clip(strengthened(drawn, jax.random.fold_in(own_key, 3), *heavy), -limit, limit).astype(held_as)


def setup_inputs(seed: int = 0) -> dict:
    arg_keys = jax.random.split(jax.random.key(seed), 8)
    return {
        "audio": draw_audio(jax.random.fold_in(arg_keys[7], 71), 0),
        "conv0_weight": bell_draw(arg_keys[1], (10, C), 10 ** -0.5, 2.0, (), jnp.float32),
        "norm_gain": jnp.clip(1.0 + 0.15 * jax.random.normal(arg_keys[2], (C,), jnp.float32), 0.25, 1.75),
        "norm_bias": bell_draw(arg_keys[3], (C,), 0.5, 3.0, (), jnp.float32),
        "conv1_weight": bell_draw(arg_keys[4], (3 * C, C), C ** -0.5, 0.25),
        "conv2_weight": bell_draw(arg_keys[5], (3 * C, C), C ** -0.5, 0.25),
        "cotangent": gaussian_with(arg_keys[6], (RECS, FRAMES, C), ((FRAMES * RECS) ** -0.5), 0.09375, ((0, 4), (1, 8)), (1, 2, 8, 2.0)),
    }


EPS = 1e-05
HIGH = lax.Precision.HIGHEST

def gelu_slope(value):
    return 0.5 * (1.0 + lax.erf(value * 0.7071067811865476)) + value * jnp.exp(-0.5 * value * value) * 0.3989422804014327

def stride_conv(active, weight):
    channels = active.shape[1]
    pairs = active.reshape(active.shape[0] // 2, 2 * channels)
    following = jnp.concatenate([pairs[1:, :channels], jnp.zeros((1, channels), active.dtype)], 0)
    output = jnp.dot(pairs, weight[:2 * channels], preferred_element_type=jnp.float32)
    output = output + jnp.dot(following, weight[2 * channels:], preferred_element_type=jnp.float32)
    return (pairs, following, output)

def weight_grad(pairs, following, delta):
    upper = jnp.dot(pairs.T, delta, preferred_element_type=jnp.float32)
    lower = jnp.dot(following.T, delta, preferred_element_type=jnp.float32)
    return jnp.concatenate([upper, lower], 0)

def stride_back(delta, weight):
    channels = delta.shape[1]
    before = jnp.concatenate([jnp.zeros((1, channels), delta.dtype), delta[:-1]], 0)
    back_pairs = jnp.dot(delta, weight[:2 * channels].T, preferred_element_type=jnp.float32)
    shifted = jnp.dot(before, weight[2 * channels:].T, preferred_element_type=jnp.float32)
    even_rows = back_pairs[:, :channels] + shifted
    return jnp.concatenate([even_rows, back_pairs[:, channels:]], 1).reshape(-1, channels)

def one_recording(samples, cotan, conv0_weight, norm_gain, norm_bias, conv1_weight, conv2_weight):
    blocks = samples.reshape(-1, 5)
    following = jnp.concatenate([blocks[1:], jnp.zeros((1, 5), blocks.dtype)], 0)
    patches = jnp.concatenate([blocks, following], 1)
    pre_norm = jnp.dot(patches, conv0_weight, precision=HIGH)
    count = pre_norm.shape[0] * 1.0
    mean = lax.optimization_barrier(jnp.sum(pre_norm, 0)) / count
    centered = pre_norm - mean
    variance = lax.optimization_barrier(jnp.sum(centered * centered, 0)) / count
    inverse = lax.rsqrt(variance + EPS)
    normed = centered * inverse
    shifted_norm = normed * norm_gain + norm_bias
    act0 = jax.nn.gelu(shifted_norm, approximate=False).astype(jnp.bfloat16)
    pairs1, follow1, pre1 = stride_conv(act0, conv1_weight)
    act1 = jax.nn.gelu(pre1, approximate=False).astype(jnp.bfloat16)
    pairs2, follow2, pre2 = stride_conv(act1, conv2_weight)
    features = jax.nn.gelu(pre2, approximate=False).astype(jnp.bfloat16)
    delta2 = (cotan.astype(jnp.float32) * gelu_slope(pre2)).astype(jnp.bfloat16)
    grad_two = weight_grad(pairs2, follow2, delta2)
    back1 = stride_back(delta2, conv2_weight)
    delta1 = (back1 * gelu_slope(pre1)).astype(jnp.bfloat16)
    grad_one = weight_grad(pairs1, follow1, delta1)
    back0 = stride_back(delta1, conv1_weight)
    dnorm = back0 * gelu_slope(shifted_norm)
    sum_one = lax.optimization_barrier(jnp.sum(dnorm, 0))
    sum_two = lax.optimization_barrier(jnp.sum(dnorm * normed, 0))
    scale = norm_gain * inverse
    dpre = scale * (dnorm - sum_one / count - normed * (sum_two / count))
    grad_zero = jnp.dot(patches.T, dpre, precision=HIGH)
    return (features, grad_zero, sum_two, sum_one, grad_one, grad_two)

def reference(audio, conv0_weight, norm_gain, norm_bias, conv1_weight, conv2_weight, cotangent):

    def step(pair):
        return one_recording(pair[0], pair[1], conv0_weight, norm_gain, norm_bias, conv1_weight, conv2_weight)
    outs = lax.map(step, (audio, cotangent))
    features = outs[0]
    grad_conv0 = lax.optimization_barrier(jnp.sum(outs[1], 0))
    grad_gain = lax.optimization_barrier(jnp.sum(outs[2], 0))
    grad_bias = lax.optimization_barrier(jnp.sum(outs[3], 0))
    grad_conv1 = lax.optimization_barrier(jnp.sum(outs[4], 0))
    grad_conv2 = lax.optimization_barrier(jnp.sum(outs[5], 0))
    return (features, grad_conv0, grad_gain, grad_bias, grad_conv1, grad_conv2)
```

```python
import functools

import jax
import jax.numpy as jnp
from jax import lax
from jax.experimental import pallas as pl
from jax.experimental.pallas import tpu as pltpu
from jax.sharding import PartitionSpec as P

EPS = 1e-05
HIGH = lax.Precision.HIGHEST
MESH = pl.DeviceIdType.MESH
F32, BF16 = jnp.float32, jnp.bfloat16
EDGE = 16
STEP = 16
PARTS = 6
PLANS = {1: 'zp'}
ORDER = (
    2, 1, 6, 2, 1, 0, 5, 4, 0, 3, 6, 6, 3, 2, 5, 4, 6, 0, 6, 6, 6, 2, 6, 3,
    1, 6, 6, 6, 0, 6, 5, 6, 2, 3, 1, 4, 0, 5, 2, 6, 3, 4, 1, 0, 5, 6, 3, 4,
    5, 1, 4,
)
INFO = 24


def gelu_parts(value):
    phi = 0.5 * (1.0 + lax.erf(value * 0.7071067811865476))
    slope = phi + value * jnp.exp(-0.5 * value * value) * 0.3989422804014327
    return value * phi, slope


def dot(a, b, ca, cb, precision=None):
    return lax.dot_general(
        a, b, (((ca,), (cb,)), ((), ())), precision=precision, preferred_element_type=F32
    )


def axes_of(tm, rec):
    plane = [1 << i for i in range(1, tm.bit_length() - 1)]
    return {"p": ("tm", plane), "z": ("rec", [1 << i for i in range(rec.bit_length() - 1)])}


def plan(tm, rec, rows):
    axes, plans = axes_of(tm, rec), []
    for part in range(PARTS):
        size, stages = rows, []
        for name in PLANS.get(part, "pz"):
            axis, bits = axes[name]
            members = 1 << len(bits)
            whole = size // members < 16 or size % (16 * members) != 0
            size = size if whole else size // members
            stages.append((axis, bits, members, size, whole))
        plans.append(stages)
    return plans


def recv_rows(stages, rows):
    return rows + sum(size * members for _, _, members, size, _ in stages)


def kernel(
    tm, rec, audio_hbm, taps_hbm, gain_hbm, bias_hbm, w1_hbm, w2_hbm, cot_hbm,
    features_ref, res_ref, small_ref,
    audio_ref, taps_ref, gain_ref, bias_ref, cot_ref, gram_ref, lhs_ref, wide_ref, info_ref, info_in,
    norm_ref, slope0_ref, act0_ref, pre1_ref, slope1_ref, act1_ref, pre2_ref, delta2_ref, delta1_ref,
    xx_ref, edge_ref, dn_ref, t0_ref, t1_ref, gf_ref, corebuf, sendbuf, recvbuf, lit_ref, lit_core, lit_xy, lit_z,
    w1_ref, w2_ref, load_sem, ed_send, ed_recv, in_send, in_recv, co_send, co_recv, rs_send, rs_recv, ag_send, ag_recv,
    sm_send, sm_recv,
):
    me = {"tm": lax.axis_index("tm"), "rec": lax.axis_index("rec")}
    rows_all, C = pre2_ref.shape
    H = C // 2
    rows = rows_all - EDGE
    count = 4.0 * rows * tm
    inside = 4.0 * rows - 1.0
    part_rows = gf_ref.shape[1]
    plans = plan(tm, rec, part_rows)
    core = lax.rem(me["tm"], 2)
    sibling = {"tm": me["tm"] + 1 - 2 * core}

    def bit_of(axis, bit):
        return lax.rem(me[axis] // bit, 2)

    def place(axis, bits, mask=0):
        where = 0
        for i, bit in enumerate(bits):
            own = bit_of(axis, bit)
            where = where + ((1 - own) if mask >> i & 1 else own) * (1 << i)
        return where

    def partner(axis, bits, mask):
        index = me[axis]
        for i, bit in enumerate(bits):
            if mask >> i & 1:
                index = index + bit * (1 - 2 * bit_of(axis, bit))
        return {axis: index}

    loads = [
        pltpu.make_async_copy(source, target, load_sem.at[i])
        for i, (source, target) in enumerate((
            (audio_hbm, audio_ref), (taps_hbm, taps_ref), (gain_hbm, gain_ref), (bias_hbm, bias_ref),
            (cot_hbm, cot_ref), (w1_hbm, w1_ref), (w2_hbm, w2_ref),
        ))
    ]
    for load in loads:
        load.start()
    barrier = pltpu.get_barrier_semaphore()
    for d in range(1, tm):
        pl.semaphore_signal(barrier, inc=1, device_id={"tm": lax.rem(me["tm"] + d, tm)}, device_id_type=MESH)
    for d in range(1, rec):
        pl.semaphore_signal(barrier, inc=1, device_id={"rec": lax.rem(me["rec"] + d, rec)}, device_id_type=MESH)

    loads[0].wait()
    groups = rows // 32
    blocks = [audio_ref[pl.ds(k, groups, stride=5), :] for k in range(5)]
    blocks.append(pltpu.roll(blocks[0], groups - 1, 0))
    lane = lax.broadcasted_iota(jnp.int32, (groups, 128), 1)
    for s in range(32):
        k, off = divmod(20 * s, 128)
        piece = blocks[k]
        if off:
            piece = pltpu.roll(piece, 128 - off, 1)
        if off + 25 > 128:
            piece = jnp.where(lane < 128 - off, piece, pltpu.roll(blocks[k + 1], 128 - off, 1))
        xx_ref[pl.ds(s, groups, stride=32), :] = jnp.where(lane < 25, piece, 0.0)
    shift = jnp.sum(jnp.sum(audio_ref[...], 0, keepdims=True), 1, keepdims=True) / (20.0 * rows)
    x = xx_ref[:rows, :]
    lane = lax.broadcasted_iota(jnp.int32, x.shape, 1)
    row = lax.broadcasted_iota(jnp.int32, x.shape, 0)
    level = x - shift
    last = jnp.logical_and(jnp.logical_and(lane >= 32, lane < 42), row < rows - 1)
    level = jnp.where(lane < 20, level, jnp.where(last, pltpu.roll(level, 17, 1), jnp.where(lane == 64, 1.0, 0.0)))
    gram_ref[...] = dot(level, level, 0, 0, HIGH)
    lane16 = lax.broadcasted_iota(jnp.int32, (16, 128), 1)
    gram, column, line = 0.0, 0.0, 0.0
    ones_row = gram_ref[64:65, :]
    for k in (0, 5, 10, 32):
        piece = gram_ref[k : k + 16, :]
        column = column + piece[:, 64:65]
        gram = gram + (pltpu.roll(piece, 128 - k, 1) if k else piece)
        line = line + (pltpu.roll(ones_row, 128 - k, 1) if k else ones_row)
    info_ref[:16, :] = jnp.where(lane16 < 10, gram, jnp.where(lane16 == 10, column, 0.0))
    info_ref[16:17, :] = line
    info_ref[17:18, :] = xx_ref[0:1, :]
    info_ref[18:19, :] = xx_ref[rows - 1 : rows, :]
    info_ref[19:20, :] = jnp.broadcast_to(shift, (1, 128))
    info_ref[20:, :] = jnp.zeros((INFO - 20, 128), F32)
    info_in[0] = info_ref[...]
    loads[4].wait()

    pl.semaphore_wait(barrier, tm - 1 + rec - 1)
    infos = []
    for d in range(1, tm):
        copy = pltpu.make_async_remote_copy(
            src_ref=info_ref, dst_ref=info_in.at[d], send_sem=in_send.at[d], recv_sem=in_recv.at[d],
            device_id={"tm": lax.rem(me["tm"] + d, tm)}, device_id_type=MESH,
        )
        copy.start()
        infos.append(copy)
    edge_copy = pltpu.make_async_remote_copy(
        src_ref=cot_ref.at[rows - 16 : rows, :], dst_ref=edge_ref, send_sem=ed_send, recv_sem=ed_recv,
        device_id={"tm": lax.rem(me["tm"] + 1, tm)}, device_id_type=MESH,
    )
    edge_copy.start()

    loads[1].wait()
    loads[2].wait()
    loads[3].wait()
    taps = taps_ref[...]
    padded = jnp.concatenate([taps, jnp.zeros((22, C), F32)], 0)
    for q in range(4):
        lanes = slice(q * C, (q + 1) * C)
        value = pltpu.roll(padded, 5 * q, 0) if q else padded
        one = value.astype(BF16)
        rest = value - one.astype(F32)
        two = rest.astype(BF16)
        three = (rest - two.astype(F32)).astype(BF16)
        for i, term in enumerate((one, two, one, two, three, one)):
            wide_ref[32 * i : 32 * (i + 1), lanes] = term
        wide_ref[192:, lanes] = jnp.zeros((64, C), BF16)

    def first_conv(begin, end):
        value = xx_ref[begin:end, :]
        one = value.astype(BF16).astype(F32)
        rest = value - one
        two = rest.astype(BF16).astype(F32)
        three = rest - two
        lhs_ref[begin:end, :128] = (
            one + pltpu.roll(one, 32, 1) + pltpu.roll(two, 64, 1) + pltpu.roll(two, 96, 1)
        ).astype(BF16)
        lhs_ref[begin:end, 128:] = (one + pltpu.roll(three, 32, 1)).astype(BF16)
        norm_ref[begin:end, :] = dot(lhs_ref[begin:end, :], wide_ref[...], 1, 0)

    first_conv(0, rows - 16)
    for copy in infos:
        copy.wait_recv()

    center = info_in[0, 19:20, :]
    for d in range(1, tm):
        center = center + info_in[d, 19:20, :]
    center = center / tm
    gram, column, line = 0.0, 0.0, 0.0
    for d in range(tm):
        off = info_in[d, 19:20, :] - center
        piece, own_line = info_in[d, :16, :], info_in[d, 16:17, :]
        own_column = piece[:, 10:11]
        gram = gram + piece + off * (own_column + own_line + inside * off)
        column = column + own_column + inside * off[:, :1]
        line = line + own_line + inside * off
    ends, starts = info_in[:, 18, :], info_in[:, 17, :]
    lane = lax.broadcasted_iota(jnp.int32, ends.shape, 1)
    slot = lax.broadcasted_iota(jnp.int32, ends.shape, 0)
    starts = jnp.where(slot == lax.rem(me["tm"] + 1, tm), 0.0, pltpu.roll(pltpu.roll(starts, 5, 1), 1, 0))
    cross = jnp.where(lane < 5, pltpu.roll(ends, 113, 1), starts) - center
    cross = jnp.where(lane < 10, cross, jnp.where(lane == 10, 1.0, 0.0))
    extra = dot(cross, cross, 0, 0, HIGH)
    gram = gram + extra[:16, :]
    column = (column + extra[:16, 10:11]) / count
    line = (line + extra[10:11, :]) / count
    spread = gram / count - column * line
    taps16 = padded[:16, :]
    through = spread[:, 0:1] * taps[0:1, :]
    for j in range(1, 10):
        through = through + spread[:, j : j + 1] * taps[j : j + 1, :]
    variance = jnp.maximum(jnp.sum(taps16 * through, 0, keepdims=True), 0.0)
    mean = jnp.sum(taps16 * (column + center[:, :1]), 0, keepdims=True)
    inverse = lax.rsqrt(variance + EPS)
    gain, bias = gain_ref[...], bias_ref[...]

    lane = lax.broadcasted_iota(jnp.int32, (16, 128), 1)
    row = lax.broadcasted_iota(jnp.int32, (16, 128), 0)
    after = jnp.where(me["tm"] == tm - 1, 0.0, info_in[tm - 1, 17:18, :])
    before = jnp.where(me["tm"] == 0, 0.0, info_in[1, 18:19, :])
    before = jnp.where(lane[:1] < 20, before, pltpu.roll(info_ref[17:18, :], 20, 1))
    tail = xx_ref[rows - 16 : rows, :]
    fill = jnp.logical_and(row == 15, jnp.logical_and(lane >= 20, lane < 25))
    xx_ref[rows - 16 : rows, :] = jnp.where(fill, pltpu.roll(after, 20, 1), tail)
    xx_ref[rows:, :] = jnp.where(
        lane < 25, jnp.where(row == 0, after, jnp.where(row == 15, before, 0.0)), 0.0
    )
    first_conv(rows - 16, rows_all)

    def first_act(i, carry):
        at = pl.ds(pl.multiple_of(i * STEP, STEP), STEP)
        row = i * STEP + lax.broadcasted_iota(jnp.int32, (STEP, C), 0)
        past = jnp.logical_and(row == rows, me["tm"] == tm - 1)
        for q in range(4):
            lanes = slice(q * C, (q + 1) * C)
            normed = (norm_ref[at, lanes] - mean) * inverse
            norm_ref[at, lanes] = normed
            act, slope = gelu_parts(normed * gain + bias)
            act0_ref[at, lanes] = jnp.where(past, 0.0, act).astype(BF16)
            slope0_ref[at, lanes] = slope
        return carry

    lax.fori_loop(0, rows_all // STEP, first_act, 0)
    act0_ref[:, 4 * C :] = pltpu.roll(act0_ref[:, :C].astype(F32), rows_all - 1, 0).astype(BF16)

    loads[5].wait()
    pre1_ref[:, :C] = dot(act0_ref[:, : 3 * C], w1_ref[...], 1, 0)
    pre1_ref[:, C:] = dot(act0_ref[:, 2 * C :], w1_ref[...], 1, 0)

    def second_act(i, carry):
        at = pl.ds(pl.multiple_of(i * STEP, STEP), STEP)
        row = i * STEP + lax.broadcasted_iota(jnp.int32, (STEP, 2 * C), 0)
        past = jnp.logical_and(row == rows, me["tm"] == tm - 1)
        act, slope = gelu_parts(pre1_ref[at, :])
        act1_ref[at, : 2 * C] = jnp.where(past, 0.0, act).astype(BF16)
        slope1_ref[at, :] = slope
        return carry

    lax.fori_loop(0, rows_all // STEP, second_act, 0)
    act1_ref[:, 2 * C :] = pltpu.roll(act1_ref[:, :C].astype(F32), rows_all - 1, 0).astype(BF16)

    loads[6].wait()
    pre2_ref[...] = dot(act1_ref[...], w2_ref[...], 1, 0)

    def third_act(i, carry):
        at = pl.ds(pl.multiple_of(i * STEP, STEP), STEP)
        act, slope = gelu_parts(pre2_ref[at, :])
        features_ref[at, :] = act.astype(BF16)
        delta2_ref[at, :] = (cot_ref[at, :].astype(F32) * slope).astype(BF16)
        return carry

    lax.fori_loop(0, rows // STEP, third_act, 0)
    edge_copy.wait_recv()
    slope = gelu_parts(pre2_ref[rows:, :])[1]
    edge = jnp.where(me["tm"] == 0, 0.0, edge_ref[...].astype(F32))
    delta2_ref[rows:, :] = (edge * slope).astype(BF16)

    state = [
        {"size": part_rows, "start": 0, "used": part_rows, "step": 0, "wait": [], "sent": [], "bases": [0], "kept": []}
        for _ in range(PARTS)
    ]

    def combine(target, offset, part, start, size, began, bases):
        block = min(32, size)

        def body(i, carry):
            at = pl.ds(pl.multiple_of(start + i * block, 16), block)
            value = gf_ref[part, at, :]
            for base in bases:
                came = pl.ds(pl.multiple_of(base + (start - began) + i * block, 16), block)
                value = value + recvbuf[part, came, :].astype(F32)
            to = pl.ds(pl.multiple_of(offset + start + i * block, 16), block)
            target[to, :] = value.astype(target.dtype)
            return carry

        lax.fori_loop(0, size // block, body, 0)

    def settle(part, start, size, base, members):
        block = min(32, size)

        def body(i, carry):
            value = 0.0
            for slot in range(members):
                came = pl.ds(pl.multiple_of(base + slot * size + i * block, 16), block)
                value = value + recvbuf[part, came, :].astype(F32)
            gf_ref[part, pl.ds(pl.multiple_of(start + i * block, 16), block), :] = value
            return carry

        lax.fori_loop(0, size // block, body, 0)

    def start_core(part, value):
        corebuf[part] = value.astype(BF16)
        copy = pltpu.make_async_remote_copy(
            src_ref=corebuf.at[part], dst_ref=recvbuf.at[part, pl.ds(0, part_rows), :],
            send_sem=co_send.at[part, 0], recv_sem=co_recv.at[part, 0], device_id=sibling, device_id_type=MESH,
        )
        copy.start()
        state[part]["wait"] = [copy]
        state[part]["sent"].append(copy)

    def advance(part):
        s, stages = state[part], plans[part]
        step = s["step"]
        s["step"] += 1
        for copy in s["wait"]:
            copy.wait_recv()
        s["wait"] = []
        size, start = s["size"], s["start"]
        if step <= len(stages) and step > 0 and stages[step - 1][4]:
            settle(part, start, size, s["bases"][0], stages[step - 1][2])
            s["bases"] = []
        if step < len(stages):
            axis, bits, members, out, whole = stages[step]
            here = place(axis, bits)
            base = s["used"]
            for mask in range(1, members):
                there = place(axis, bits, mask)
                if whole:
                    away = start
                    if mask == 1:
                        combine(sendbuf.at[part], 0, part, start, size, start, s["bases"])
                        own = pl.ds(pl.multiple_of(base + here * size, 16), size)
                        recvbuf[part, own, :] = sendbuf[part, pl.ds(pl.multiple_of(start, 16), size), :]
                    to = base + here * size
                else:
                    away = start + there * out
                    combine(sendbuf.at[part], 0, part, away, out, start, s["bases"])
                    to = base + (mask - 1) * out
                copy = pltpu.make_async_remote_copy(
                    src_ref=sendbuf.at[part, pl.ds(pl.multiple_of(away, 16), out), :],
                    dst_ref=recvbuf.at[part, pl.ds(pl.multiple_of(to, 16), out), :],
                    send_sem=rs_send.at[part, step, mask], recv_sem=rs_recv.at[part, step, mask],
                    device_id=partner(axis, bits, mask), device_id_type=MESH,
                )
                copy.start()
                s["wait"].append(copy)
                s["sent"].append(copy)
            if whole:
                s["bases"] = [base]
                s["kept"].append(None)
            else:
                keep = start + here * out
                combine(gf_ref.at[part], 0, part, keep, out, start, s["bases"])
                s["bases"] = [base + i * out for i in range(members - 1)]
                s["kept"].append((keep, out))
                s["start"] = keep
            s["size"], s["used"] = out, base + members * out
            return
        if step == len(stages):
            combine(res_ref.at[core], part * part_rows, part, start, size, start, s["bases"])
        back = 2 * len(stages) - 1 - step
        while back >= 0 and s["kept"][back] is None:
            back -= 1
            s["step"] += 1
        if back >= 0:
            axis, bits, members, _, _ = stages[back]
            keep, out = s["kept"][back]
            piece = res_ref.at[core, pl.ds(pl.multiple_of(part * part_rows + keep, 16), out), :]
            for mask in range(1, members):
                copy = pltpu.make_async_remote_copy(
                    src_ref=piece, dst_ref=piece,
                    send_sem=ag_send.at[part, back, mask], recv_sem=ag_recv.at[part, back, mask],
                    device_id=partner(axis, bits, mask), device_id_type=MESH,
                )
                copy.start()
                s["wait"].append(copy)
                s["sent"].append(copy)
        elif back == -1:
            piece = res_ref.at[core, pl.ds(part * part_rows, part_rows), :]
            copy = pltpu.make_async_remote_copy(
                src_ref=piece, dst_ref=piece, send_sem=co_send.at[part, 1], recv_sem=co_recv.at[part, 1],
                device_id=sibling, device_id_type=MESH,
            )
            copy.start()
            s["wait"].append(copy)
            s["sent"].append(copy)

    mine = pl.ds(pl.multiple_of(core * H, H), H)
    other = pl.ds(pl.multiple_of((1 - core) * H, H), H)
    half = PARTS // 2

    def weight_grad(part, lanes):
        begin = (part % half) * part_rows
        one = slice(begin, begin + part_rows)
        two = slice(2 * C + begin, 2 * C + begin + part_rows)
        if part < half:
            return dot(act1_ref[:rows, one], delta2_ref[:rows, lanes], 0, 0)
        first, second = delta1_ref.at[:rows, :C], delta1_ref.at[:rows, C:]
        return dot(act0_ref[:rows, one], first[:, lanes], 0, 0) + dot(act0_ref[:rows, two], second[:, lanes], 0, 0)

    def advance_part(part):
        step = state[part]["step"]
        if step == 0 and not state[part]["sent"]:
            start_core(part, weight_grad(part, other))
            return
        if step == 0:
            gf_ref[part] = weight_grad(part, mine)
        if step <= 2 * len(plans[part]) + 2:
            advance(part)

    def second_delta():
        t0_ref[...] = dot(delta2_ref[...], w2_ref[...], 1, 1)
        even = t0_ref[:, :C] + pltpu.roll(t0_ref[:, 2 * C :], 1, 0)
        delta1_ref[:, :C] = (even * slope1_ref[:, :C]).astype(BF16)
        delta1_ref[:, C:] = (t0_ref[:, C : 2 * C] * slope1_ref[:, C:]).astype(BF16)

    def even_back():
        t0_ref[...] = dot(delta1_ref[:, :C], w1_ref[...], 1, 1)

    def odd_back():
        t1_ref[...] = dot(delta1_ref[:, C:], w1_ref[...], 1, 1)
        t1_ref[:, 2 * C :] = pltpu.roll(t1_ref[:, 2 * C :], 1, 0)

    zero = jnp.zeros((STEP, C), F32)

    def back(i, carry):
        one, two = carry
        at = pl.ds(pl.multiple_of(i * STEP, STEP), STEP)
        grads = (
            t0_ref[at, :C] + t1_ref[at, 2 * C :],
            t0_ref[at, C : 2 * C],
            t0_ref[at, 2 * C :] + t1_ref[at, :C],
            t1_ref[at, C : 2 * C],
        )
        for q in range(4):
            lanes = slice(q * C, (q + 1) * C)
            dnorm = grads[q] * slope0_ref[at, lanes]
            dn_ref[at, lanes] = dnorm
            one = one + dnorm
            two = two + dnorm * norm_ref[at, lanes]
        return one, two

    sums = {"both": (zero, zero), "taps": jnp.zeros((32, C), F32)}
    quarter = rows // STEP // 4

    def back_rows(i):
        sums["both"] = lax.fori_loop(i * quarter, (i + 1) * quarter, back, sums["both"])

    def taps_of(q):
        samples = xx_ref[:rows, :] - center
        total = dot(samples[:, :32], dn_ref[:, q * C : (q + 1) * C], 0, 0, HIGH)
        sums["taps"] = sums["taps"] + (pltpu.roll(total, 32 - 5 * q, 0) if q else total)

    def small_grads():
        local_one, local_two = (jnp.sum(value, 0, keepdims=True) for value in sums["both"])
        grad_zero = (gain * inverse) * (sums["taps"][:16] - local_one * column - (local_two * inverse) * through)
        row = lax.broadcasted_iota(jnp.int32, (16, C), 0)
        little = jnp.where(row < 10, grad_zero, jnp.where(row == 10, local_two, jnp.where(row == 11, local_one, 0.0)))
        lit_ref[0], lit_ref[1] = little[:, :H], little[:, H:]

    plane, z = (axes_of(tm, rec)[name] for name in "pz")
    small_state = {"wait": [], "sent": [], "step": 0}

    def send_small(source, target, group, device):
        copy = pltpu.make_async_remote_copy(
            src_ref=source, dst_ref=target, send_sem=sm_send.at[group], recv_sem=sm_recv.at[group],
            device_id=device, device_id_type=MESH,
        )
        copy.start()
        small_state["wait"].append(copy)
        small_state["sent"].append(copy)

    def spread_small(buffer, axis, bits, first_sem):
        here = buffer.at[place(axis, bits)]
        for mask in range(1, 1 << len(bits)):
            send_small(here, here, first_sem + mask, partner(axis, bits, mask))

    def total_of(buffer):
        total = buffer[0]
        for i in range(1, buffer.shape[0]):
            total = total + buffer[i]
        return total

    def advance_small():
        step = small_state["step"]
        small_state["step"] += 1
        for copy in small_state["wait"]:
            copy.wait_recv()
        small_state["wait"] = []
        if step == 0:
            send_small(lit_ref.at[1 - core], lit_core, 0, sibling)
        elif step == 1:
            lit_xy[place(*plane)] = lit_ref[core] + lit_core[...]
            spread_small(lit_xy, *plane, 0)
        elif step == 2:
            lit_z[place(*z)] = total_of(lit_xy)
            spread_small(lit_z, *z, lit_xy.shape[0])
        elif step == 3:
            small_ref[core] = total_of(lit_z)
            send_small(small_ref.at[core], small_ref.at[core], lit_xy.shape[0] + lit_z.shape[0], sibling)

    def first_small():
        small_grads()
        advance_small()

    main = [second_delta, even_back, odd_back]
    main += [functools.partial(back_rows, i) for i in range(4)] + [functools.partial(taps_of, q) for q in range(4)]
    main += [first_small] + [advance_small] * 4
    for item in ORDER:
        if item < PARTS:
            advance_part(item)
        elif main:
            main.pop(0)()
    for work in main:
        work()
    while min(s["step"] - 2 * len(p) for s, p in zip(state, plans)) < 3:
        for part in range(PARTS):
            advance_part(part)
    for s in state:
        for copy in s["sent"]:
            copy.wait_send()
    for copy in small_state["sent"] + infos + [edge_copy]:
        copy.wait_send()


def finish(
    features_ref, res_ref, small_ref, features_hbm, zero_hbm, gain_hbm, bias_hbm, one_hbm, two_hbm,
    wide_ref, zero_ref, gain_ref, bias_ref, sem,
):
    H = res_ref.shape[2]
    per = one_hbm.shape[0]
    copies = []

    def send(source, target):
        copy = pltpu.make_async_copy(source, target, sem.at[len(copies)])
        copy.start()
        copies.append(copy)

    send(features_ref, features_hbm)
    for h in range(2):
        lanes = slice(h * H, (h + 1) * H)
        zero_ref[:, lanes] = small_ref[h, :10, :]
        gain_ref[:, lanes] = small_ref[h, 10:11, :]
        bias_ref[:, lanes] = small_ref[h, 11:12, :]
    send(zero_ref, zero_hbm)
    send(gain_ref, gain_hbm)
    send(bias_ref, bias_hbm)
    chunk = per // 4
    for i in range(8):
        at = slice(i * chunk, (i + 1) * chunk)
        for h in range(2):
            wide_ref[at, h * H : (h + 1) * H] = res_ref[h, at, :].astype(F32)
        target = two_hbm if i < 4 else one_hbm
        begin = (i % 4) * chunk
        send(wide_ref.at[at, :], target.at[begin : begin + chunk, :])
    for copy in copies:
        copy.wait()


def shards(tm, rec, audio, conv0_weight, norm_gain, norm_bias, conv1_weight, conv2_weight, cotangent):
    samples = audio.shape[1]
    rows = samples // 20
    rows_all = rows + EDGE
    C = conv0_weight.shape[1]
    H = C // 2
    total_rows = 6 * C
    part_rows = total_rows // PARTS
    plans = plan(tm, rec, part_rows)
    received = max(recv_rows(stages, part_rows) for stages in plans)
    most = max(members for stages in plans for _, _, members, _, _ in stages)
    stages = len(plans[0])
    chips = tm // 2
    vmem = pl.BlockSpec(memory_space=pltpu.VMEM)
    hbm = pl.BlockSpec(memory_space=pltpu.HBM)
    dma = pltpu.SemaphoreType.DMA
    features, res, small = pl.pallas_call(
        functools.partial(kernel, tm, rec),
        out_shape=(
            jax.ShapeDtypeStruct((rows, C), BF16),
            jax.ShapeDtypeStruct((2, total_rows, H), BF16),
            jax.ShapeDtypeStruct((2, 16, H), F32),
        ),
        in_specs=[hbm] * 7,
        out_specs=(vmem,) * 3,
        scratch_shapes=[
            pltpu.VMEM((samples // 128, 128), F32),
            pltpu.VMEM((10, C), F32),
            pltpu.VMEM((1, C), F32),
            pltpu.VMEM((1, C), F32),
            pltpu.VMEM((rows, C), BF16),
            pltpu.VMEM((128, 128), F32),
            pltpu.VMEM((rows_all, 256), BF16),
            pltpu.VMEM((256, 4 * C), BF16),
            pltpu.VMEM((INFO, 128), F32),
            pltpu.VMEM((tm, INFO, 128), F32),
            pltpu.VMEM((rows_all, 4 * C), F32),
            pltpu.VMEM((rows_all, 4 * C), F32),
            pltpu.VMEM((rows_all, 5 * C), BF16),
            pltpu.VMEM((rows_all, 2 * C), F32),
            pltpu.VMEM((rows_all, 2 * C), F32),
            pltpu.VMEM((rows_all, 3 * C), BF16),
            pltpu.VMEM((rows_all, C), F32),
            pltpu.VMEM((rows_all, C), BF16),
            pltpu.VMEM((rows_all, 2 * C), BF16),
            pltpu.VMEM((rows_all, 128), F32),
            pltpu.VMEM((EDGE, C), BF16),
            pltpu.VMEM((rows, 4 * C), F32),
            pltpu.VMEM((rows_all, 3 * C), F32),
            pltpu.VMEM((rows_all, 3 * C), F32),
            pltpu.VMEM((PARTS, part_rows, H), F32),
            pltpu.VMEM((PARTS, part_rows, H), BF16),
            pltpu.VMEM((PARTS, part_rows, H), BF16),
            pltpu.VMEM((PARTS, received, H), BF16),
            pltpu.VMEM((2, 16, H), F32),
            pltpu.VMEM((16, H), F32),
            pltpu.VMEM((chips, 16, H), F32),
            pltpu.VMEM((rec, 16, H), F32),
            pltpu.VMEM((3 * C, C), BF16),
            pltpu.VMEM((3 * C, C), BF16),
            dma((7,)),
            dma,
            dma,
            dma((tm,)),
            dma((tm,)),
            dma((PARTS, 2)),
            dma((PARTS, 2)),
            dma((PARTS, stages, most)),
            dma((PARTS, stages, most)),
            dma((PARTS, stages, most)),
            dma((PARTS, stages, most)),
            dma((chips + rec + 1,)),
            dma((chips + rec + 1,)),
        ],
        compiler_params=pltpu.CompilerParams(
            collective_id=0, has_side_effects=True, vmem_limit_bytes=44 * 2**20
        ),
    )(*(
        pltpu.with_memory_space_constraint(value, pltpu.HBM)
        for value in (
            audio.reshape(samples // 128, 128), conv0_weight, norm_gain[None, :], norm_bias[None, :],
            conv1_weight, conv2_weight, cotangent[0],
        )
    ))
    features, grad_zero, grad_gain, grad_bias, grad_one, grad_two = pl.pallas_call(
        finish,
        out_shape=(
            jax.ShapeDtypeStruct((rows, C), BF16),
            jax.ShapeDtypeStruct((10, C), F32),
            jax.ShapeDtypeStruct((1, C), F32),
            jax.ShapeDtypeStruct((1, C), F32),
            jax.ShapeDtypeStruct((3 * C, C), F32),
            jax.ShapeDtypeStruct((3 * C, C), F32),
        ),
        in_specs=[vmem] * 3,
        out_specs=(hbm,) * 6,
        scratch_shapes=[
            pltpu.VMEM((total_rows, C), F32),
            pltpu.VMEM((10, C), F32),
            pltpu.VMEM((1, C), F32),
            pltpu.VMEM((1, C), F32),
            dma((12,)),
        ],
        compiler_params=pltpu.CompilerParams(vmem_limit_bytes=24 * 2**20),
    )(features, res, small)
    return (features[None], grad_zero, grad_gain[0], grad_bias[0], grad_one, grad_two)


def solution(mesh):
    return jax.shard_map(
        functools.partial(shards, mesh.shape["tm"], mesh.shape["rec"]),
        mesh=mesh,
        in_specs=(P("rec", "tm"), P(), P(), P(), P(), P(), P("rec", "tm", None)),
        out_specs=(P("rec", "tm", None), P(), P(), P(), P(), P()),
        check_vma=False,
    )
```

```python
import functools

import jax
import jax.numpy as jnp
from jax import lax
from jax.experimental import pallas as pl
from jax.experimental.pallas import tpu as pltpu
from jax.sharding import PartitionSpec as P

EPS = 1e-05
HIGH = lax.Precision.HIGHEST
MESH = pl.DeviceIdType.MESH
F32, BF16 = jnp.float32, jnp.bfloat16
EDGE = 16
STEP = 16
PARTS = 6
PLANS = {2: 'zp'}
ORDER = (
    1, 2, 6, 1, 2, 4, 0, 0, 6, 4, 6, 1, 6, 6, 5, 3, 6, 6, 6, 5, 0, 2, 6, 1,
    3, 6, 4, 6, 6, 0, 6, 5, 1, 4, 3, 2, 0, 5, 6, 4, 1, 3, 2, 5, 0, 6, 4, 3,
    5, 2, 3,
)
INFO = 24


def gelu_parts(value):
    phi = 0.5 * (1.0 + lax.erf(value * 0.7071067811865476))
    slope = phi + value * jnp.exp(-0.5 * value * value) * 0.3989422804014327
    return value * phi, slope


def dot(a, b, ca, cb, precision=None):
    return lax.dot_general(
        a, b, (((ca,), (cb,)), ((), ())), precision=precision, preferred_element_type=F32
    )


def axes_of(tm, rec):
    plane = [1 << i for i in range(1, tm.bit_length() - 1)]
    return {"p": ("tm", plane), "z": ("rec", [1 << i for i in range(rec.bit_length() - 1)])}


def plan(tm, rec, rows):
    axes, plans = axes_of(tm, rec), []
    for part in range(PARTS):
        size, stages = rows, []
        for name in PLANS.get(part, "pz"):
            axis, bits = axes[name]
            members = 1 << len(bits)
            whole = size // members < 16 or size % (16 * members) != 0
            size = size if whole else size // members
            stages.append((axis, bits, members, size, whole))
        plans.append(stages)
    return plans


def recv_rows(stages, rows):
    return rows + sum(size * members for _, _, members, size, _ in stages)


def kernel(
    tm, rec, audio_hbm, taps_hbm, gain_hbm, bias_hbm, w1_hbm, w2_hbm, cot_hbm,
    features_ref, res_ref, small_ref,
    audio_ref, taps_ref, gain_ref, bias_ref, cot_ref, gram_ref, lhs_ref, wide_ref, info_ref, info_in,
    norm_ref, phi0_ref, act0_ref, slope1_ref, act1_ref, delta2_ref, delta1_ref,
    xx_ref, dn_ref, t0_ref, t1_ref, gf_ref, corebuf, sendbuf, recvbuf, lit_ref, lit_core, lit_xy, lit_z,
    w1_ref, w2_ref, load_sem, ed_send, ed_recv, in_send, in_recv, co_send, co_recv, rs_send, rs_recv, ag_send, ag_recv,
    sm_send, sm_recv,
):
    me = {"tm": lax.axis_index("tm"), "rec": lax.axis_index("rec")}
    rows_all, C = delta2_ref.shape
    H = C // 2
    rows = rows_all - EDGE
    count = 4.0 * rows * tm
    inside = 4.0 * rows - 1.0
    part_rows = gf_ref.shape[1]
    plans = plan(tm, rec, part_rows)
    core = lax.rem(me["tm"], 2)
    sibling = {"tm": me["tm"] + 1 - 2 * core}

    def bit_of(axis, bit):
        return lax.rem(me[axis] // bit, 2)

    def place(axis, bits, mask=0):
        where = 0
        for i, bit in enumerate(bits):
            own = bit_of(axis, bit)
            where = where + ((1 - own) if mask >> i & 1 else own) * (1 << i)
        return where

    def partner(axis, bits, mask):
        index = me[axis]
        for i, bit in enumerate(bits):
            if mask >> i & 1:
                index = index + bit * (1 - 2 * bit_of(axis, bit))
        return {axis: index}

    loads = [
        pltpu.make_async_copy(source, target, load_sem.at[i])
        for i, (source, target) in enumerate((
            (audio_hbm, audio_ref), (taps_hbm, taps_ref), (gain_hbm, gain_ref), (bias_hbm, bias_ref),
            (cot_hbm, cot_ref.at[:rows, :]), (w1_hbm, w1_ref), (w2_hbm, w2_ref),
        ))
    ]
    loads[0].start()
    barrier = pltpu.get_barrier_semaphore()
    for d in range(1, tm):
        pl.semaphore_signal(barrier, inc=1, device_id={"tm": lax.rem(me["tm"] + d, tm)}, device_id_type=MESH)
    for d in range(1, rec):
        pl.semaphore_signal(barrier, inc=1, device_id={"rec": lax.rem(me["rec"] + d, rec)}, device_id_type=MESH)

    for load in loads[1:]:
        load.start()

    loads[0].wait()
    groups = rows // 32
    blocks = [audio_ref[pl.ds(k, groups, stride=5), :] for k in range(5)]
    blocks.append(pltpu.roll(blocks[0], groups - 1, 0))
    lane = lax.broadcasted_iota(jnp.int32, (groups, 128), 1)
    for s in range(32):
        k, off = divmod(20 * s, 128)
        piece = blocks[k]
        if off:
            piece = pltpu.roll(piece, 128 - off, 1)
        if off + 25 > 128:
            piece = jnp.where(lane < 128 - off, piece, pltpu.roll(blocks[k + 1], 128 - off, 1))
        xx_ref[pl.ds(s, groups, stride=32), :] = jnp.where(lane < 25, piece, 0.0)
    shift = jnp.sum(jnp.sum(audio_ref[...], 0, keepdims=True), 1, keepdims=True) / (20.0 * rows)
    x = xx_ref[:rows, :]
    lane = lax.broadcasted_iota(jnp.int32, x.shape, 1)
    row = lax.broadcasted_iota(jnp.int32, x.shape, 0)
    level = x - shift
    last = jnp.logical_and(jnp.logical_and(lane >= 32, lane < 42), row < rows - 1)
    level = jnp.where(lane < 20, level, jnp.where(last, pltpu.roll(level, 17, 1), jnp.where(lane == 64, 1.0, 0.0)))
    gram_ref[...] = dot(level, level, 0, 0, HIGH)
    lane16 = lax.broadcasted_iota(jnp.int32, (16, 128), 1)
    gram, column, line = 0.0, 0.0, 0.0
    ones_row = gram_ref[64:65, :]
    for k in (0, 5, 10, 32):
        piece = gram_ref[k : k + 16, :]
        column = column + piece[:, 64:65]
        gram = gram + (pltpu.roll(piece, 128 - k, 1) if k else piece)
        line = line + (pltpu.roll(ones_row, 128 - k, 1) if k else ones_row)
    info_ref[:16, :] = jnp.where(lane16 < 10, gram, jnp.where(lane16 == 10, column, 0.0))
    info_ref[16:17, :] = line
    info_ref[17:18, :] = xx_ref[0:1, :]
    info_ref[18:19, :] = xx_ref[rows - 1 : rows, :]
    info_ref[19:20, :] = jnp.broadcast_to(shift, (1, 128))
    info_ref[20:, :] = jnp.zeros((INFO - 20, 128), F32)
    info_in[0] = info_ref[...]
    pl.semaphore_wait(barrier, tm - 1 + rec - 1)
    infos = []
    for d in range(1, tm):
        copy = pltpu.make_async_remote_copy(
            src_ref=info_ref, dst_ref=info_in.at[d], send_sem=in_send.at[d], recv_sem=in_recv.at[d],
            device_id={"tm": lax.rem(me["tm"] + d, tm)}, device_id_type=MESH,
        )
        copy.start()
        infos.append(copy)
    loads[4].wait()
    edge_copy = pltpu.make_async_remote_copy(
        src_ref=cot_ref.at[rows - 16 : rows, :], dst_ref=cot_ref.at[rows:, :], send_sem=ed_send, recv_sem=ed_recv,
        device_id={"tm": lax.rem(me["tm"] + 1, tm)}, device_id_type=MESH,
    )
    edge_copy.start()

    loads[1].wait()
    loads[2].wait()
    loads[3].wait()
    taps = taps_ref[...]
    padded = jnp.concatenate([taps, jnp.zeros((22, C), F32)], 0)
    for q in range(4):
        lanes = slice(q * C, (q + 1) * C)
        value = pltpu.roll(padded, 5 * q, 0) if q else padded
        one = value.astype(BF16)
        rest = value - one.astype(F32)
        two = rest.astype(BF16)
        three = (rest - two.astype(F32)).astype(BF16)
        for i, term in enumerate((one, two, one, two, three, one)):
            wide_ref[32 * i : 32 * (i + 1), lanes] = term
        wide_ref[192:, lanes] = jnp.zeros((64, C), BF16)

    def first_conv(begin, end):
        value = xx_ref[begin:end, :]
        one = value.astype(BF16).astype(F32)
        rest = value - one
        two = rest.astype(BF16).astype(F32)
        three = rest - two
        lhs_ref[begin:end, :128] = (
            one + pltpu.roll(one, 32, 1) + pltpu.roll(two, 64, 1) + pltpu.roll(two, 96, 1)
        ).astype(BF16)
        lhs_ref[begin:end, 128:] = (one + pltpu.roll(three, 32, 1)).astype(BF16)
        norm_ref[begin:end, :] = dot(lhs_ref[begin:end, :], wide_ref[...], 1, 0)

    first_conv(0, rows - 16)
    for copy in infos:
        copy.wait_recv()

    center = info_in[0, 19:20, :]
    for d in range(1, tm):
        center = center + info_in[d, 19:20, :]
    center = center / tm
    gram, column, line = 0.0, 0.0, 0.0
    for d in range(tm):
        off = info_in[d, 19:20, :] - center
        piece, own_line = info_in[d, :16, :], info_in[d, 16:17, :]
        own_column = piece[:, 10:11]
        gram = gram + piece + off * (own_column + own_line + inside * off)
        column = column + own_column + inside * off[:, :1]
        line = line + own_line + inside * off
    ends, starts = info_in[:, 18, :], info_in[:, 17, :]
    lane = lax.broadcasted_iota(jnp.int32, ends.shape, 1)
    slot = lax.broadcasted_iota(jnp.int32, ends.shape, 0)
    starts = jnp.where(slot == lax.rem(me["tm"] + 1, tm), 0.0, pltpu.roll(pltpu.roll(starts, 5, 1), 1, 0))
    cross = jnp.where(lane < 5, pltpu.roll(ends, 113, 1), starts) - center
    cross = jnp.where(lane < 10, cross, jnp.where(lane == 10, 1.0, 0.0))
    extra = dot(cross, cross, 0, 0, HIGH)
    gram = gram + extra[:16, :]
    column = (column + extra[:16, 10:11]) / count
    line = (line + extra[10:11, :]) / count
    spread = gram / count - column * line
    taps16 = padded[:16, :]
    through = spread[:, 0:1] * taps[0:1, :]
    for j in range(1, 10):
        through = through + spread[:, j : j + 1] * taps[j : j + 1, :]
    variance = jnp.maximum(jnp.sum(taps16 * through, 0, keepdims=True), 0.0)
    mean = jnp.sum(taps16 * (column + center[:, :1]), 0, keepdims=True)
    inverse = lax.rsqrt(variance + EPS)
    gain, bias = gain_ref[...], bias_ref[...]

    lane = lax.broadcasted_iota(jnp.int32, (16, 128), 1)
    row = lax.broadcasted_iota(jnp.int32, (16, 128), 0)
    after = jnp.where(me["tm"] == tm - 1, 0.0, info_in[tm - 1, 17:18, :])
    before = jnp.where(me["tm"] == 0, 0.0, info_in[1, 18:19, :])
    before = jnp.where(lane[:1] < 20, before, pltpu.roll(info_ref[17:18, :], 20, 1))
    tail = xx_ref[rows - 16 : rows, :]
    fill = jnp.logical_and(row == 15, jnp.logical_and(lane >= 20, lane < 25))
    xx_ref[rows - 16 : rows, :] = jnp.where(fill, pltpu.roll(after, 20, 1), tail)
    xx_ref[rows:, :] = jnp.where(
        lane < 25, jnp.where(row == 0, after, jnp.where(row == 15, before, 0.0)), 0.0
    )
    first_conv(rows - 16, rows_all)

    def first_act(at, q):
        lanes = slice(q * C, (q + 1) * C)
        normed = (norm_ref[at, lanes] - mean) * inverse
        norm_ref[at, lanes] = normed
        shifted = normed * gain + bias
        phi = 0.5 * (1.0 + lax.erf(shifted * 0.7071067811865476))
        act0_ref[at, lanes] = (shifted * phi).astype(BF16)
        phi0_ref[at, lanes] = phi

    def first_rows(i, carry):
        for q in range(4):
            first_act(pl.ds(pl.multiple_of(i * STEP, STEP), STEP), q)
        return carry

    lax.fori_loop(0, rows_all // STEP, first_rows, 0)

    @pl.when(me["tm"] == tm - 1)
    def _():
        row = lax.broadcasted_iota(jnp.int32, (EDGE, 4 * C), 0)
        act0_ref[rows:, : 4 * C] = jnp.where(row == 0, 0.0, act0_ref[rows:, : 4 * C].astype(F32)).astype(BF16)

    act0_ref[:, 4 * C :] = pltpu.roll(act0_ref[:, :C].astype(F32), rows_all - 1, 0).astype(BF16)

    loads[5].wait()

    def second_act(half, block):
        lanes = slice(half * C + block * H, half * C + (block + 1) * H)
        value = dot(act0_ref[:, 2 * half * C : (2 * half + 3) * C], w1_ref[:, block * H : (block + 1) * H], 1, 0)
        act, slope = gelu_parts(value)
        act1_ref[:, lanes] = act.astype(BF16)
        slope1_ref[:, lanes] = slope

    second_act(0, 0)
    second_act(0, 1)
    second_act(1, 0)
    second_act(1, 1)

    @pl.when(me["tm"] == tm - 1)
    def _():
        row = lax.broadcasted_iota(jnp.int32, (EDGE, 2 * C), 0)
        act1_ref[rows:, : 2 * C] = jnp.where(row == 0, 0.0, act1_ref[rows:, : 2 * C].astype(F32)).astype(BF16)

    act1_ref[:, 2 * C :] = pltpu.roll(act1_ref[:, :C].astype(F32), rows_all - 1, 0).astype(BF16)

    loads[6].wait()
    edge_copy.wait_recv()

    @pl.when(me["tm"] == 0)
    def _():
        cot_ref[rows:, :] = jnp.zeros((EDGE, C), BF16)

    for block in range(2):
        lanes = slice(block * H, (block + 1) * H)
        act, slope = gelu_parts(dot(act1_ref[...], w2_ref[:, lanes], 1, 0))
        features_ref[:, lanes] = act[:rows].astype(BF16)
        delta2_ref[:, lanes] = (cot_ref[:, lanes].astype(F32) * slope).astype(BF16)

    state = [
        {"size": part_rows, "start": 0, "used": part_rows, "step": 0, "wait": [], "sent": [], "bases": [0], "kept": []}
        for _ in range(PARTS)
    ]

    def combine(target, offset, part, start, size, began, bases):
        block = min(32, size)

        def body(i, carry):
            at = pl.ds(pl.multiple_of(start + i * block, 16), block)
            value = gf_ref[part, at, :]
            for base in bases:
                came = pl.ds(pl.multiple_of(base + (start - began) + i * block, 16), block)
                value = value + recvbuf[part, came, :].astype(F32)
            to = pl.ds(pl.multiple_of(offset + start + i * block, 16), block)
            target[to, :] = value.astype(target.dtype)
            return carry

        lax.fori_loop(0, size // block, body, 0)

    def settle(part, start, size, base, members):
        block = min(32, size)

        def body(i, carry):
            value = 0.0
            for slot in range(members):
                came = pl.ds(pl.multiple_of(base + slot * size + i * block, 16), block)
                value = value + recvbuf[part, came, :].astype(F32)
            gf_ref[part, pl.ds(pl.multiple_of(start + i * block, 16), block), :] = value
            return carry

        lax.fori_loop(0, size // block, body, 0)

    def start_core(part, value):
        corebuf[part] = value.astype(BF16)
        copy = pltpu.make_async_remote_copy(
            src_ref=corebuf.at[part], dst_ref=recvbuf.at[part, pl.ds(0, part_rows), :],
            send_sem=co_send.at[part, 0], recv_sem=co_recv.at[part, 0], device_id=sibling, device_id_type=MESH,
        )
        copy.start()
        state[part]["wait"] = [copy]
        state[part]["sent"].append(copy)

    def advance(part):
        s, stages = state[part], plans[part]
        step = s["step"]
        s["step"] += 1
        for copy in s["wait"]:
            copy.wait_recv()
        s["wait"] = []
        size, start = s["size"], s["start"]
        if step <= len(stages) and step > 0 and stages[step - 1][4]:
            settle(part, start, size, s["bases"][0], stages[step - 1][2])
            s["bases"] = []
        if step < len(stages):
            axis, bits, members, out, whole = stages[step]
            here = place(axis, bits)
            base = s["used"]
            for mask in range(members - 1, 0, -1):
                there = place(axis, bits, mask)
                if whole:
                    away = start
                    if mask == members - 1:
                        combine(sendbuf.at[part], 0, part, start, size, start, s["bases"])
                        own = pl.ds(pl.multiple_of(base + here * size, 16), size)
                        recvbuf[part, own, :] = sendbuf[part, pl.ds(pl.multiple_of(start, 16), size), :]
                    to = base + here * size
                else:
                    away = start + there * out
                    combine(sendbuf.at[part], 0, part, away, out, start, s["bases"])
                    to = base + (mask - 1) * out
                copy = pltpu.make_async_remote_copy(
                    src_ref=sendbuf.at[part, pl.ds(pl.multiple_of(away, 16), out), :],
                    dst_ref=recvbuf.at[part, pl.ds(pl.multiple_of(to, 16), out), :],
                    send_sem=rs_send.at[part, step, mask], recv_sem=rs_recv.at[part, step, mask],
                    device_id=partner(axis, bits, mask), device_id_type=MESH,
                )
                copy.start()
                s["wait"].append(copy)
                s["sent"].append(copy)
            if whole:
                s["bases"] = [base]
                s["kept"].append(None)
            else:
                keep = start + here * out
                combine(gf_ref.at[part], 0, part, keep, out, start, s["bases"])
                s["bases"] = [base + i * out for i in range(members - 1)]
                s["kept"].append((keep, out))
                s["start"] = keep
            s["size"], s["used"] = out, base + members * out
            return
        if step == len(stages):
            combine(res_ref.at[core], part * part_rows, part, start, size, start, s["bases"])
        back = 2 * len(stages) - 1 - step
        while back >= 0 and s["kept"][back] is None:
            back -= 1
            s["step"] += 1
        if back >= 0:
            axis, bits, members, _, _ = stages[back]
            keep, out = s["kept"][back]
            piece = res_ref.at[core, pl.ds(pl.multiple_of(part * part_rows + keep, 16), out), :]
            for mask in range(members - 1, 0, -1):
                copy = pltpu.make_async_remote_copy(
                    src_ref=piece, dst_ref=piece,
                    send_sem=ag_send.at[part, back, mask], recv_sem=ag_recv.at[part, back, mask],
                    device_id=partner(axis, bits, mask), device_id_type=MESH,
                )
                copy.start()
                s["wait"].append(copy)
                s["sent"].append(copy)
        elif back == -1:
            piece = res_ref.at[core, pl.ds(part * part_rows, part_rows), :]
            copy = pltpu.make_async_remote_copy(
                src_ref=piece, dst_ref=piece, send_sem=co_send.at[part, 1], recv_sem=co_recv.at[part, 1],
                device_id=sibling, device_id_type=MESH,
            )
            copy.start()
            s["wait"].append(copy)
            s["sent"].append(copy)

    mine = pl.ds(pl.multiple_of(core * H, H), H)
    other = pl.ds(pl.multiple_of((1 - core) * H, H), H)
    half = PARTS // 2

    def weight_grad(part, lanes):
        begin = (part % half) * part_rows
        one = slice(begin, begin + part_rows)
        two = slice(2 * C + begin, 2 * C + begin + part_rows)
        if part < half:
            return dot(act1_ref[:rows, one], delta2_ref[:rows, lanes], 0, 0)
        first, second = delta1_ref.at[:rows, :C], delta1_ref.at[:rows, C:]
        return dot(act0_ref[:rows, one], first[:, lanes], 0, 0) + dot(act0_ref[:rows, two], second[:, lanes], 0, 0)

    def advance_part(part):
        step = state[part]["step"]
        if step == 0 and not state[part]["sent"]:
            start_core(part, weight_grad(part, other))
            return
        if step == 0:
            gf_ref[part] = weight_grad(part, mine)
        if step <= 2 * len(plans[part]) + 2:
            advance(part)

    def second_delta():
        t0_ref[...] = dot(delta2_ref[...], w2_ref[...], 1, 1)
        even = t0_ref[:, :C] + pltpu.roll(t0_ref[:, 2 * C :], 1, 0)
        delta1_ref[:, :C] = (even * slope1_ref[:, :C]).astype(BF16)
        delta1_ref[:, C:] = (t0_ref[:, C : 2 * C] * slope1_ref[:, C:]).astype(BF16)

    def even_back():
        t0_ref[...] = dot(delta1_ref[:, :C], w1_ref[...], 1, 1)

    def odd_back():
        t1_ref[...] = dot(delta1_ref[:, C:], w1_ref[...], 1, 1)
        t1_ref[:, 2 * C :] = pltpu.roll(t1_ref[:, 2 * C :], 1, 0)

    zero = jnp.zeros((STEP, C), F32)

    def back(i, carry):
        one, two = carry
        at = pl.ds(pl.multiple_of(i * STEP, STEP), STEP)
        grads = (
            t0_ref[at, :C] + t1_ref[at, 2 * C :],
            t0_ref[at, C : 2 * C],
            t0_ref[at, 2 * C :] + t1_ref[at, :C],
            t1_ref[at, C : 2 * C],
        )
        for q in range(4):
            lanes = slice(q * C, (q + 1) * C)
            normed = norm_ref[at, lanes]
            shifted = normed * gain + bias
            slope = phi0_ref[at, lanes] + shifted * jnp.exp(-0.5 * shifted * shifted) * 0.3989422804014327
            dnorm = grads[q] * slope
            dn_ref[at, lanes] = dnorm
            one = one + dnorm
            two = two + dnorm * normed
        return one, two

    sums = {"both": (zero, zero), "taps": jnp.zeros((32, C), F32)}
    quarter = rows // STEP // 4

    def back_rows(i):
        sums["both"] = lax.fori_loop(i * quarter, (i + 1) * quarter, back, sums["both"])

    def taps_of(q):
        samples = xx_ref[:rows, :] - center
        total = dot(samples[:, :32], dn_ref[:, q * C : (q + 1) * C], 0, 0, HIGH)
        sums["taps"] = sums["taps"] + (pltpu.roll(total, 32 - 5 * q, 0) if q else total)

    def small_grads():
        local_one, local_two = (jnp.sum(value, 0, keepdims=True) for value in sums["both"])
        grad_zero = (gain * inverse) * (sums["taps"][:16] - local_one * column - (local_two * inverse) * through)
        row = lax.broadcasted_iota(jnp.int32, (16, C), 0)
        little = jnp.where(row < 10, grad_zero, jnp.where(row == 10, local_two, jnp.where(row == 11, local_one, 0.0)))
        lit_ref[0], lit_ref[1] = little[:, :H], little[:, H:]

    plane, z = (axes_of(tm, rec)[name] for name in "pz")
    small_state = {"wait": [], "sent": [], "step": 0}

    def send_small(source, target, group, device):
        copy = pltpu.make_async_remote_copy(
            src_ref=source, dst_ref=target, send_sem=sm_send.at[group], recv_sem=sm_recv.at[group],
            device_id=device, device_id_type=MESH,
        )
        copy.start()
        small_state["wait"].append(copy)
        small_state["sent"].append(copy)

    def spread_small(buffer, axis, bits, first_sem):
        here = buffer.at[place(axis, bits)]
        for mask in range(1, 1 << len(bits)):
            send_small(here, here, first_sem + mask, partner(axis, bits, mask))

    def total_of(buffer):
        total = buffer[0]
        for i in range(1, buffer.shape[0]):
            total = total + buffer[i]
        return total

    def advance_small():
        step = small_state["step"]
        small_state["step"] += 1
        for copy in small_state["wait"]:
            copy.wait_recv()
        small_state["wait"] = []
        if step == 0:
            send_small(lit_ref.at[1 - core], lit_core, 0, sibling)
        elif step == 1:
            lit_xy[place(*plane)] = lit_ref[core] + lit_core[...]
            spread_small(lit_xy, *plane, 0)
        elif step == 2:
            lit_z[place(*z)] = total_of(lit_xy)
            spread_small(lit_z, *z, lit_xy.shape[0])
        elif step == 3:
            small_ref[core] = total_of(lit_z)
            send_small(small_ref.at[core], small_ref.at[core], lit_xy.shape[0] + lit_z.shape[0], sibling)

    def first_small():
        small_grads()
        advance_small()

    main = [second_delta, even_back, odd_back]
    main += [functools.partial(back_rows, i) for i in range(4)] + [functools.partial(taps_of, q) for q in range(4)]
    main += [first_small] + [advance_small] * 4
    for item in ORDER:
        if item < PARTS:
            advance_part(item)
        elif main:
            main.pop(0)()
    for work in main:
        work()
    while min(s["step"] - 2 * len(p) for s, p in zip(state, plans)) < 3:
        for part in range(PARTS):
            advance_part(part)
    for s in state:
        for copy in s["sent"]:
            copy.wait_send()
    for copy in small_state["sent"] + infos + [edge_copy]:
        copy.wait_send()


def finish(
    features_ref, res_ref, small_ref, features_hbm, zero_hbm, gain_hbm, bias_hbm, one_hbm, two_hbm,
    wide_ref, zero_ref, gain_ref, bias_ref, sem,
):
    H = res_ref.shape[2]
    per = one_hbm.shape[0]
    copies = []

    def send(source, target):
        copy = pltpu.make_async_copy(source, target, sem.at[len(copies)])
        copy.start()
        copies.append(copy)

    send(features_ref, features_hbm)
    for h in range(2):
        lanes = slice(h * H, (h + 1) * H)
        zero_ref[:, lanes] = small_ref[h, :10, :]
        gain_ref[:, lanes] = small_ref[h, 10:11, :]
        bias_ref[:, lanes] = small_ref[h, 11:12, :]
    send(zero_ref, zero_hbm)
    send(gain_ref, gain_hbm)
    send(bias_ref, bias_hbm)
    chunk = per // 4
    for i in range(8):
        at = slice(i * chunk, (i + 1) * chunk)
        for h in range(2):
            wide_ref[at, h * H : (h + 1) * H] = res_ref[h, at, :].astype(F32)
        target = two_hbm if i < 4 else one_hbm
        begin = (i % 4) * chunk
        send(wide_ref.at[at, :], target.at[begin : begin + chunk, :])
    for copy in copies:
        copy.wait()


def shards(tm, rec, audio, conv0_weight, norm_gain, norm_bias, conv1_weight, conv2_weight, cotangent):
    samples = audio.shape[1]
    rows = samples // 20
    rows_all = rows + EDGE
    C = conv0_weight.shape[1]
    H = C // 2
    total_rows = 6 * C
    part_rows = total_rows // PARTS
    plans = plan(tm, rec, part_rows)
    received = max(recv_rows(stages, part_rows) for stages in plans)
    most = max(members for stages in plans for _, _, members, _, _ in stages)
    stages = len(plans[0])
    chips = tm // 2
    vmem = pl.BlockSpec(memory_space=pltpu.VMEM)
    hbm = pl.BlockSpec(memory_space=pltpu.HBM)
    dma = pltpu.SemaphoreType.DMA
    features, res, small = pl.pallas_call(
        functools.partial(kernel, tm, rec),
        out_shape=(
            jax.ShapeDtypeStruct((rows, C), BF16),
            jax.ShapeDtypeStruct((2, total_rows, H), BF16),
            jax.ShapeDtypeStruct((2, 16, H), F32),
        ),
        in_specs=[hbm] * 7,
        out_specs=(vmem,) * 3,
        scratch_shapes=[
            pltpu.VMEM((samples // 128, 128), F32),
            pltpu.VMEM((10, C), F32),
            pltpu.VMEM((1, C), F32),
            pltpu.VMEM((1, C), F32),
            pltpu.VMEM((rows_all, C), BF16),
            pltpu.VMEM((128, 128), F32),
            pltpu.VMEM((rows_all, 256), BF16),
            pltpu.VMEM((256, 4 * C), BF16),
            pltpu.VMEM((INFO, 128), F32),
            pltpu.VMEM((tm, INFO, 128), F32),
            pltpu.VMEM((rows_all, 4 * C), F32),
            pltpu.VMEM((rows_all, 4 * C), F32),
            pltpu.VMEM((rows_all, 5 * C), BF16),
            pltpu.VMEM((rows_all, 2 * C), F32),
            pltpu.VMEM((rows_all, 3 * C), BF16),
            pltpu.VMEM((rows_all, C), BF16),
            pltpu.VMEM((rows_all, 2 * C), BF16),
            pltpu.VMEM((rows_all, 128), F32),
            pltpu.VMEM((rows, 4 * C), F32),
            pltpu.VMEM((rows_all, 3 * C), F32),
            pltpu.VMEM((rows_all, 3 * C), F32),
            pltpu.VMEM((PARTS, part_rows, H), F32),
            pltpu.VMEM((PARTS, part_rows, H), BF16),
            pltpu.VMEM((PARTS, part_rows, H), BF16),
            pltpu.VMEM((PARTS, received, H), BF16),
            pltpu.VMEM((2, 16, H), F32),
            pltpu.VMEM((16, H), F32),
            pltpu.VMEM((chips, 16, H), F32),
            pltpu.VMEM((rec, 16, H), F32),
            pltpu.VMEM((3 * C, C), BF16),
            pltpu.VMEM((3 * C, C), BF16),
            dma((7,)),
            dma,
            dma,
            dma((tm,)),
            dma((tm,)),
            dma((PARTS, 2)),
            dma((PARTS, 2)),
            dma((PARTS, stages, most)),
            dma((PARTS, stages, most)),
            dma((PARTS, stages, most)),
            dma((PARTS, stages, most)),
            dma((chips + rec + 1,)),
            dma((chips + rec + 1,)),
        ],
        compiler_params=pltpu.CompilerParams(
            collective_id=0, has_side_effects=True, vmem_limit_bytes=44 * 2**20
        ),
    )(*(
        pltpu.with_memory_space_constraint(value, pltpu.HBM)
        for value in (
            audio.reshape(samples // 128, 128), conv0_weight, norm_gain[None, :], norm_bias[None, :],
            conv1_weight, conv2_weight, cotangent[0],
        )
    ))
    features, grad_zero, grad_gain, grad_bias, grad_one, grad_two = pl.pallas_call(
        finish,
        out_shape=(
            jax.ShapeDtypeStruct((rows, C), BF16),
            jax.ShapeDtypeStruct((10, C), F32),
            jax.ShapeDtypeStruct((1, C), F32),
            jax.ShapeDtypeStruct((1, C), F32),
            jax.ShapeDtypeStruct((3 * C, C), F32),
            jax.ShapeDtypeStruct((3 * C, C), F32),
        ),
        in_specs=[vmem] * 3,
        out_specs=(hbm,) * 6,
        scratch_shapes=[
            pltpu.VMEM((total_rows, C), F32),
            pltpu.VMEM((10, C), F32),
            pltpu.VMEM((1, C), F32),
            pltpu.VMEM((1, C), F32),
            dma((12,)),
        ],
        compiler_params=pltpu.CompilerParams(vmem_limit_bytes=24 * 2**20),
    )(features, res, small)
    return (features[None], grad_zero, grad_gain[0], grad_bias[0], grad_one, grad_two)


def solution(mesh):
    return jax.shard_map(
        functools.partial(shards, mesh.shape["tm"], mesh.shape["rec"]),
        mesh=mesh,
        in_specs=(P("rec", "tm"), P(), P(), P(), P(), P(), P("rec", "tm", None)),
        out_specs=(P("rec", "tm", None), P(), P(), P(), P(), P()),
        check_vma=False,
    )
```

```python
import functools

import jax
import jax.numpy as jnp
from jax import lax
from jax.experimental import pallas as pl
from jax.experimental.pallas import tpu as pltpu
from jax.sharding import PartitionSpec as P

EPS = 1e-05
HIGH = lax.Precision.HIGHEST
MESH = pl.DeviceIdType.MESH
F32, BF16 = jnp.float32, jnp.bfloat16
EDGE = 16
STEP = 16
PARTS = 6
PLANS = {2: 'zp'}
ORDER = (
    1, 2, 6, 1, 2, 4, 0, 0, 6, 4, 6, 1, 6, 6, 5, 3, 6, 6, 6, 5, 0, 2, 6, 1,
    3, 6, 4, 6, 6, 0, 6, 5, 1, 4, 3, 2, 0, 5, 6, 4, 1, 3, 2, 5, 0, 6, 4, 3,
    5, 2, 3,
)
INFO = 24


def gelu_parts(value):
    phi = 0.5 * (1.0 + lax.erf(value * 0.7071067811865476))
    slope = phi + value * jnp.exp(-0.5 * value * value) * 0.3989422804014327
    return value * phi, slope


def dot(a, b, ca, cb, precision=None):
    return lax.dot_general(
        a, b, (((ca,), (cb,)), ((), ())), precision=precision, preferred_element_type=F32
    )


def axes_of(tm, rec):
    plane = [1 << i for i in range(1, tm.bit_length() - 1)]
    return {"p": ("tm", plane), "z": ("rec", [1 << i for i in range(rec.bit_length() - 1)])}


def plan(tm, rec, rows):
    axes, plans = axes_of(tm, rec), []
    for part in range(PARTS):
        size, stages = rows, []
        for name in PLANS.get(part, "pz"):
            axis, bits = axes[name]
            members = 1 << len(bits)
            whole = size // members < 16 or size % (16 * members) != 0
            size = size if whole else size // members
            stages.append((axis, bits, members, size, whole))
        plans.append(stages)
    return plans


def recv_rows(stages, rows):
    return rows + sum(size * members for _, _, members, size, _ in stages)


def kernel(
    tm, rec, audio_hbm, taps_hbm, gain_hbm, bias_hbm, w1_hbm, w2_hbm, cot_hbm,
    features_ref, res_ref, small_ref,
    audio_ref, taps_ref, gain_ref, bias_ref, cot_ref, gram_ref, lhs_ref, wide_ref, info_ref, info_in,
    norm_ref, act0_ref, slope1_ref, act1_ref, delta2_ref, delta1_ref,
    xx_ref, dn_ref, t0_ref, t1_ref, gf_ref, corebuf, sendbuf, recvbuf, lit_ref, lit_core, lit_xy, lit_z,
    w1_ref, w2_ref, load_sem, ed_send, ed_recv, in_send, in_recv, co_send, co_recv, rs_send, rs_recv, ag_send, ag_recv,
    sm_send, sm_recv,
):
    me = {"tm": lax.axis_index("tm"), "rec": lax.axis_index("rec")}
    rows_all, C = delta2_ref.shape
    H = C // 2
    rows = rows_all - EDGE
    count = 4.0 * rows * tm
    inside = 4.0 * rows - 1.0
    part_rows = gf_ref.shape[1]
    plans = plan(tm, rec, part_rows)
    core = lax.rem(me["tm"], 2)
    sibling = {"tm": me["tm"] + 1 - 2 * core}

    def bit_of(axis, bit):
        return lax.rem(me[axis] // bit, 2)

    def place(axis, bits, mask=0):
        where = 0
        for i, bit in enumerate(bits):
            own = bit_of(axis, bit)
            where = where + ((1 - own) if mask >> i & 1 else own) * (1 << i)
        return where

    def partner(axis, bits, mask):
        index = me[axis]
        for i, bit in enumerate(bits):
            if mask >> i & 1:
                index = index + bit * (1 - 2 * bit_of(axis, bit))
        return {axis: index}

    loads = [
        pltpu.make_async_copy(source, target, load_sem.at[i])
        for i, (source, target) in enumerate((
            (audio_hbm, audio_ref), (taps_hbm, taps_ref), (gain_hbm, gain_ref), (bias_hbm, bias_ref),
            (cot_hbm, cot_ref.at[:rows, :]), (w1_hbm, w1_ref), (w2_hbm, w2_ref),
        ))
    ]
    loads[0].start()
    barrier = pltpu.get_barrier_semaphore()
    for d in range(1, tm):
        pl.semaphore_signal(barrier, inc=1, device_id={"tm": lax.rem(me["tm"] + d, tm)}, device_id_type=MESH)
    for d in range(1, rec):
        pl.semaphore_signal(barrier, inc=1, device_id={"rec": lax.rem(me["rec"] + d, rec)}, device_id_type=MESH)

    for load in loads[1:]:
        load.start()

    loads[0].wait()
    groups = rows // 32
    blocks = [audio_ref[pl.ds(k, groups, stride=5), :] for k in range(5)]
    blocks.append(pltpu.roll(blocks[0], groups - 1, 0))
    lane = lax.broadcasted_iota(jnp.int32, (groups, 128), 1)
    for s in range(32):
        k, off = divmod(20 * s, 128)
        piece = blocks[k]
        if off:
            piece = pltpu.roll(piece, 128 - off, 1)
        if off + 25 > 128:
            piece = jnp.where(lane < 128 - off, piece, pltpu.roll(blocks[k + 1], 128 - off, 1))
        xx_ref[pl.ds(s, groups, stride=32), :] = jnp.where(lane < 25, piece, 0.0)
    shift = jnp.sum(jnp.sum(audio_ref[...], 0, keepdims=True), 1, keepdims=True) / (20.0 * rows)
    x = xx_ref[:rows, :]
    lane = lax.broadcasted_iota(jnp.int32, x.shape, 1)
    row = lax.broadcasted_iota(jnp.int32, x.shape, 0)
    level = x - shift
    last = jnp.logical_and(jnp.logical_and(lane >= 32, lane < 42), row < rows - 1)
    level = jnp.where(lane < 20, level, jnp.where(last, pltpu.roll(level, 17, 1), jnp.where(lane == 64, 1.0, 0.0)))
    gram_ref[...] = dot(level, level, 0, 0, HIGH)
    lane16 = lax.broadcasted_iota(jnp.int32, (16, 128), 1)
    gram, column, line = 0.0, 0.0, 0.0
    ones_row = gram_ref[64:65, :]
    for k in (0, 5, 10, 32):
        piece = gram_ref[k : k + 16, :]
        column = column + piece[:, 64:65]
        gram = gram + (pltpu.roll(piece, 128 - k, 1) if k else piece)
        line = line + (pltpu.roll(ones_row, 128 - k, 1) if k else ones_row)
    info_ref[:16, :] = jnp.where(lane16 < 10, gram, jnp.where(lane16 == 10, column, 0.0))
    info_ref[16:17, :] = line
    info_ref[17:18, :] = xx_ref[0:1, :]
    info_ref[18:19, :] = xx_ref[rows - 1 : rows, :]
    info_ref[19:20, :] = jnp.broadcast_to(shift, (1, 128))
    info_ref[20:, :] = jnp.zeros((INFO - 20, 128), F32)
    info_in[0] = info_ref[...]
    pl.semaphore_wait(barrier, tm - 1 + rec - 1)
    infos = []
    for d in range(1, tm):
        copy = pltpu.make_async_remote_copy(
            src_ref=info_ref, dst_ref=info_in.at[d], send_sem=in_send.at[d], recv_sem=in_recv.at[d],
            device_id={"tm": lax.rem(me["tm"] + d, tm)}, device_id_type=MESH,
        )
        copy.start()
        infos.append(copy)
    loads[4].wait()
    edge_copy = pltpu.make_async_remote_copy(
        src_ref=cot_ref.at[rows - 16 : rows, :], dst_ref=cot_ref.at[rows:, :], send_sem=ed_send, recv_sem=ed_recv,
        device_id={"tm": lax.rem(me["tm"] + 1, tm)}, device_id_type=MESH,
    )
    edge_copy.start()

    loads[1].wait()
    loads[2].wait()
    loads[3].wait()
    taps = taps_ref[...]
    padded = jnp.concatenate([taps, jnp.zeros((22, C), F32)], 0)
    for q in range(4):
        lanes = slice(q * C, (q + 1) * C)
        value = pltpu.roll(padded, 5 * q, 0) if q else padded
        one = value.astype(BF16)
        rest = value - one.astype(F32)
        two = rest.astype(BF16)
        three = (rest - two.astype(F32)).astype(BF16)
        for i, term in enumerate((one, two, one, two, three, one)):
            wide_ref[32 * i : 32 * (i + 1), lanes] = term
        wide_ref[192:, lanes] = jnp.zeros((64, C), BF16)

    def first_conv(begin, end):
        value = xx_ref[begin:end, :]
        one = value.astype(BF16).astype(F32)
        rest = value - one
        two = rest.astype(BF16).astype(F32)
        three = rest - two
        lhs_ref[begin:end, :128] = (
            one + pltpu.roll(one, 32, 1) + pltpu.roll(two, 64, 1) + pltpu.roll(two, 96, 1)
        ).astype(BF16)
        lhs_ref[begin:end, 128:] = (one + pltpu.roll(three, 32, 1)).astype(BF16)
        norm_ref[begin:end, :] = dot(lhs_ref[begin:end, :], wide_ref[...], 1, 0)

    first_conv(0, rows - 16)
    for copy in infos:
        copy.wait_recv()

    center = info_in[0, 19:20, :]
    for d in range(1, tm):
        center = center + info_in[d, 19:20, :]
    center = center / tm
    gram, column, line = 0.0, 0.0, 0.0
    for d in range(tm):
        off = info_in[d, 19:20, :] - center
        piece, own_line = info_in[d, :16, :], info_in[d, 16:17, :]
        own_column = piece[:, 10:11]
        gram = gram + piece + off * (own_column + own_line + inside * off)
        column = column + own_column + inside * off[:, :1]
        line = line + own_line + inside * off
    ends, starts = info_in[:, 18, :], info_in[:, 17, :]
    lane = lax.broadcasted_iota(jnp.int32, ends.shape, 1)
    slot = lax.broadcasted_iota(jnp.int32, ends.shape, 0)
    starts = jnp.where(slot == lax.rem(me["tm"] + 1, tm), 0.0, pltpu.roll(pltpu.roll(starts, 5, 1), 1, 0))
    cross = jnp.where(lane < 5, pltpu.roll(ends, 113, 1), starts) - center
    cross = jnp.where(lane < 10, cross, jnp.where(lane == 10, 1.0, 0.0))
    extra = dot(cross, cross, 0, 0, HIGH)
    gram = gram + extra[:16, :]
    column = (column + extra[:16, 10:11]) / count
    line = (line + extra[10:11, :]) / count
    spread = gram / count - column * line
    taps16 = padded[:16, :]
    through = spread[:, 0:1] * taps[0:1, :]
    for j in range(1, 10):
        through = through + spread[:, j : j + 1] * taps[j : j + 1, :]
    variance = jnp.maximum(jnp.sum(taps16 * through, 0, keepdims=True), 0.0)
    mean = jnp.sum(taps16 * (column + center[:, :1]), 0, keepdims=True)
    inverse = lax.rsqrt(variance + EPS)
    gain, bias = gain_ref[...], bias_ref[...]

    lane = lax.broadcasted_iota(jnp.int32, (16, 128), 1)
    row = lax.broadcasted_iota(jnp.int32, (16, 128), 0)
    after = jnp.where(me["tm"] == tm - 1, 0.0, info_in[tm - 1, 17:18, :])
    before = jnp.where(me["tm"] == 0, 0.0, info_in[1, 18:19, :])
    before = jnp.where(lane[:1] < 20, before, pltpu.roll(info_ref[17:18, :], 20, 1))
    tail = xx_ref[rows - 16 : rows, :]
    fill = jnp.logical_and(row == 15, jnp.logical_and(lane >= 20, lane < 25))
    xx_ref[rows - 16 : rows, :] = jnp.where(fill, pltpu.roll(after, 20, 1), tail)
    xx_ref[rows:, :] = jnp.where(
        lane < 25, jnp.where(row == 0, after, jnp.where(row == 15, before, 0.0)), 0.0
    )
    first_conv(rows - 16, rows_all)

    scale = gain * inverse

    def first_act(at, q):
        lanes = slice(q * C, (q + 1) * C)
        shifted = (norm_ref[at, lanes] - mean) * scale + bias
        act0_ref[at, lanes] = (shifted * (0.5 * (1.0 + lax.erf(shifted * 0.7071067811865476)))).astype(BF16)

    def first_rows(i, carry):
        for q in range(4):
            first_act(pl.ds(pl.multiple_of(i * STEP, STEP), STEP), q)
        return carry

    lax.fori_loop(0, rows_all // STEP, first_rows, 0)

    @pl.when(me["tm"] == tm - 1)
    def _():
        row = lax.broadcasted_iota(jnp.int32, (EDGE, 4 * C), 0)
        act0_ref[rows:, : 4 * C] = jnp.where(row == 0, 0.0, act0_ref[rows:, : 4 * C].astype(F32)).astype(BF16)

    act0_ref[:, 4 * C :] = pltpu.roll(act0_ref[:, :C].astype(F32), rows_all - 1, 0).astype(BF16)

    loads[5].wait()

    def second_act(half, block):
        lanes = slice(half * C + block * H, half * C + (block + 1) * H)
        value = dot(act0_ref[:, 2 * half * C : (2 * half + 3) * C], w1_ref[:, block * H : (block + 1) * H], 1, 0)
        act, slope = gelu_parts(value)
        act1_ref[:, lanes] = act.astype(BF16)
        slope1_ref[:, lanes] = slope

    second_act(0, 0)
    second_act(0, 1)
    second_act(1, 0)
    second_act(1, 1)

    @pl.when(me["tm"] == tm - 1)
    def _():
        row = lax.broadcasted_iota(jnp.int32, (EDGE, 2 * C), 0)
        act1_ref[rows:, : 2 * C] = jnp.where(row == 0, 0.0, act1_ref[rows:, : 2 * C].astype(F32)).astype(BF16)

    act1_ref[:, 2 * C :] = pltpu.roll(act1_ref[:, :C].astype(F32), rows_all - 1, 0).astype(BF16)

    loads[6].wait()
    edge_copy.wait_recv()

    @pl.when(me["tm"] == 0)
    def _():
        cot_ref[rows:, :] = jnp.zeros((EDGE, C), BF16)

    mine = pl.ds(pl.multiple_of(core * H, H), H)
    other = pl.ds(pl.multiple_of((1 - core) * H, H), H)

    def third_act(lanes, value):
        act, slope = gelu_parts(value)
        features_ref[:, lanes] = act[:rows].astype(BF16)
        delta2_ref[:, lanes] = (cot_ref[:, lanes].astype(F32) * slope).astype(BF16)

    theirs = dot(act1_ref[...], w2_ref[:, other], 1, 0)
    own = dot(act1_ref[...], w2_ref[:, mine], 1, 0)
    third_act(other, theirs)

    state = [
        {"size": part_rows, "start": 0, "used": part_rows, "step": 0, "wait": [], "sent": [], "bases": [0], "kept": []}
        for _ in range(PARTS)
    ]

    def combine(target, offset, part, start, size, began, bases):
        block = min(32, size)

        def body(i, carry):
            at = pl.ds(pl.multiple_of(start + i * block, 16), block)
            value = gf_ref[part, at, :]
            for base in bases:
                came = pl.ds(pl.multiple_of(base + (start - began) + i * block, 16), block)
                value = value + recvbuf[part, came, :].astype(F32)
            to = pl.ds(pl.multiple_of(offset + start + i * block, 16), block)
            target[to, :] = value.astype(target.dtype)
            return carry

        lax.fori_loop(0, size // block, body, 0)

    def settle(part, start, size, base, members):
        block = min(32, size)

        def body(i, carry):
            value = 0.0
            for slot in range(members):
                came = pl.ds(pl.multiple_of(base + slot * size + i * block, 16), block)
                value = value + recvbuf[part, came, :].astype(F32)
            gf_ref[part, pl.ds(pl.multiple_of(start + i * block, 16), block), :] = value
            return carry

        lax.fori_loop(0, size // block, body, 0)

    def start_core(part, value):
        corebuf[part] = value.astype(BF16)
        copy = pltpu.make_async_remote_copy(
            src_ref=corebuf.at[part], dst_ref=recvbuf.at[part, pl.ds(0, part_rows), :],
            send_sem=co_send.at[part, 0], recv_sem=co_recv.at[part, 0], device_id=sibling, device_id_type=MESH,
        )
        copy.start()
        state[part]["wait"] = [copy]
        state[part]["sent"].append(copy)

    def advance(part):
        s, stages = state[part], plans[part]
        step = s["step"]
        s["step"] += 1
        for copy in s["wait"]:
            copy.wait_recv()
        s["wait"] = []
        size, start = s["size"], s["start"]
        if step <= len(stages) and step > 0 and stages[step - 1][4]:
            settle(part, start, size, s["bases"][0], stages[step - 1][2])
            s["bases"] = []
        if step < len(stages):
            axis, bits, members, out, whole = stages[step]
            here = place(axis, bits)
            base = s["used"]
            for mask in range(members - 1, 0, -1):
                there = place(axis, bits, mask)
                if whole:
                    away = start
                    if mask == members - 1:
                        combine(sendbuf.at[part], 0, part, start, size, start, s["bases"])
                        own = pl.ds(pl.multiple_of(base + here * size, 16), size)
                        recvbuf[part, own, :] = sendbuf[part, pl.ds(pl.multiple_of(start, 16), size), :]
                    to = base + here * size
                else:
                    away = start + there * out
                    combine(sendbuf.at[part], 0, part, away, out, start, s["bases"])
                    to = base + (mask - 1) * out
                copy = pltpu.make_async_remote_copy(
                    src_ref=sendbuf.at[part, pl.ds(pl.multiple_of(away, 16), out), :],
                    dst_ref=recvbuf.at[part, pl.ds(pl.multiple_of(to, 16), out), :],
                    send_sem=rs_send.at[part, step, mask], recv_sem=rs_recv.at[part, step, mask],
                    device_id=partner(axis, bits, mask), device_id_type=MESH,
                )
                copy.start()
                s["wait"].append(copy)
                s["sent"].append(copy)
            if whole:
                s["bases"] = [base]
                s["kept"].append(None)
            else:
                keep = start + here * out
                combine(gf_ref.at[part], 0, part, keep, out, start, s["bases"])
                s["bases"] = [base + i * out for i in range(members - 1)]
                s["kept"].append((keep, out))
                s["start"] = keep
            s["size"], s["used"] = out, base + members * out
            return
        if step == len(stages):
            combine(res_ref.at[core], part * part_rows, part, start, size, start, s["bases"])
        back = 2 * len(stages) - 1 - step
        while back >= 0 and s["kept"][back] is None:
            back -= 1
            s["step"] += 1
        if back >= 0:
            axis, bits, members, _, _ = stages[back]
            keep, out = s["kept"][back]
            piece = res_ref.at[core, pl.ds(pl.multiple_of(part * part_rows + keep, 16), out), :]
            for mask in range(members - 1, 0, -1):
                copy = pltpu.make_async_remote_copy(
                    src_ref=piece, dst_ref=piece,
                    send_sem=ag_send.at[part, back, mask], recv_sem=ag_recv.at[part, back, mask],
                    device_id=partner(axis, bits, mask), device_id_type=MESH,
                )
                copy.start()
                s["wait"].append(copy)
                s["sent"].append(copy)
        elif back == -1:
            piece = res_ref.at[core, pl.ds(part * part_rows, part_rows), :]
            copy = pltpu.make_async_remote_copy(
                src_ref=piece, dst_ref=piece, send_sem=co_send.at[part, 1], recv_sem=co_recv.at[part, 1],
                device_id=sibling, device_id_type=MESH,
            )
            copy.start()
            s["wait"].append(copy)
            s["sent"].append(copy)

    half = PARTS // 2

    def weight_grad(part, lanes):
        begin = (part % half) * part_rows
        one = slice(begin, begin + part_rows)
        two = slice(2 * C + begin, 2 * C + begin + part_rows)
        if part < half:
            return dot(act1_ref[:rows, one], delta2_ref[:rows, lanes], 0, 0)
        first, second = delta1_ref.at[:rows, :C], delta1_ref.at[:rows, C:]
        return dot(act0_ref[:rows, one], first[:, lanes], 0, 0) + dot(act0_ref[:rows, two], second[:, lanes], 0, 0)

    def advance_part(part):
        step = state[part]["step"]
        if step == 0 and not state[part]["sent"]:
            start_core(part, weight_grad(part, other))
            return
        if step == 0:
            gf_ref[part] = weight_grad(part, mine)
        if step <= 2 * len(plans[part]) + 2:
            advance(part)

    def second_delta():
        t0_ref[...] = dot(delta2_ref[...], w2_ref[...], 1, 1)
        even = t0_ref[:, :C] + pltpu.roll(t0_ref[:, 2 * C :], 1, 0)
        delta1_ref[:, :C] = (even * slope1_ref[:, :C]).astype(BF16)
        delta1_ref[:, C:] = (t0_ref[:, C : 2 * C] * slope1_ref[:, C:]).astype(BF16)

    def even_back():
        t0_ref[...] = dot(delta1_ref[:, :C], w1_ref[...], 1, 1)

    def odd_back():
        t1_ref[...] = dot(delta1_ref[:, C:], w1_ref[...], 1, 1)
        t1_ref[:, 2 * C :] = pltpu.roll(t1_ref[:, 2 * C :], 1, 0)

    zero = jnp.zeros((STEP, C), F32)

    def back(i, carry):
        one, two = carry
        at = pl.ds(pl.multiple_of(i * STEP, STEP), STEP)
        grads = (
            t0_ref[at, :C] + t1_ref[at, 2 * C :],
            t0_ref[at, C : 2 * C],
            t0_ref[at, 2 * C :] + t1_ref[at, :C],
            t1_ref[at, C : 2 * C],
        )
        for q in range(4):
            lanes = slice(q * C, (q + 1) * C)
            normed = (norm_ref[at, lanes] - mean) * inverse
            dnorm = grads[q] * gelu_parts(normed * gain + bias)[1]
            dn_ref[at, lanes] = dnorm
            one = one + dnorm
            two = two + dnorm * normed
        return one, two

    sums = {"both": (zero, zero), "taps": jnp.zeros((32, C), F32)}
    quarter = rows // STEP // 4

    def back_rows(i):
        sums["both"] = lax.fori_loop(i * quarter, (i + 1) * quarter, back, sums["both"])

    def taps_of(q):
        samples = xx_ref[:rows, :] - center
        total = dot(samples[:, :32], dn_ref[:, q * C : (q + 1) * C], 0, 0, HIGH)
        sums["taps"] = sums["taps"] + (pltpu.roll(total, 32 - 5 * q, 0) if q else total)

    def small_grads():
        local_one, local_two = (jnp.sum(value, 0, keepdims=True) for value in sums["both"])
        grad_zero = scale * (sums["taps"][:16] - local_one * column - (local_two * inverse) * through)
        row = lax.broadcasted_iota(jnp.int32, (16, C), 0)
        little = jnp.where(row < 10, grad_zero, jnp.where(row == 10, local_two, jnp.where(row == 11, local_one, 0.0)))
        lit_ref[0], lit_ref[1] = little[:, :H], little[:, H:]

    plane, z = (axes_of(tm, rec)[name] for name in "pz")
    small_state = {"wait": [], "sent": [], "step": 0}

    def send_small(source, target, group, device):
        copy = pltpu.make_async_remote_copy(
            src_ref=source, dst_ref=target, send_sem=sm_send.at[group], recv_sem=sm_recv.at[group],
            device_id=device, device_id_type=MESH,
        )
        copy.start()
        small_state["wait"].append(copy)
        small_state["sent"].append(copy)

    def spread_small(buffer, axis, bits, first_sem):
        here = buffer.at[place(axis, bits)]
        for mask in range(1, 1 << len(bits)):
            send_small(here, here, first_sem + mask, partner(axis, bits, mask))

    def total_of(buffer):
        total = buffer[0]
        for i in range(1, buffer.shape[0]):
            total = total + buffer[i]
        return total

    def advance_small():
        step = small_state["step"]
        small_state["step"] += 1
        for copy in small_state["wait"]:
            copy.wait_recv()
        small_state["wait"] = []
        if step == 0:
            send_small(lit_ref.at[1 - core], lit_core, 0, sibling)
        elif step == 1:
            lit_xy[place(*plane)] = lit_ref[core] + lit_core[...]
            spread_small(lit_xy, *plane, 0)
        elif step == 2:
            lit_z[place(*z)] = total_of(lit_xy)
            spread_small(lit_z, *z, lit_xy.shape[0])
        elif step == 3:
            small_ref[core] = total_of(lit_z)
            send_small(small_ref.at[core], small_ref.at[core], lit_xy.shape[0] + lit_z.shape[0], sibling)

    def first_small():
        small_grads()
        advance_small()

    main = [second_delta, even_back, odd_back]
    main += [functools.partial(back_rows, i) for i in range(4)] + [functools.partial(taps_of, q) for q in range(4)]
    main += [first_small] + [advance_small] * 4
    early = next(i for i, item in enumerate(ORDER) if item >= half or item in ORDER[:i])
    for item in ORDER[:early]:
        advance_part(item)
    third_act(mine, own)
    for item in ORDER[early:]:
        if item < PARTS:
            advance_part(item)
        elif main:
            main.pop(0)()
    for work in main:
        work()
    while min(s["step"] - 2 * len(p) for s, p in zip(state, plans)) < 3:
        for part in range(PARTS):
            advance_part(part)
    for s in state:
        for copy in s["sent"]:
            copy.wait_send()
    for copy in small_state["sent"] + infos + [edge_copy]:
        copy.wait_send()


def finish(
    features_ref, res_ref, small_ref, features_hbm, zero_hbm, gain_hbm, bias_hbm, one_hbm, two_hbm,
    wide_ref, zero_ref, gain_ref, bias_ref, sem,
):
    H = res_ref.shape[2]
    per = one_hbm.shape[0]
    copies = []

    def send(source, target):
        copy = pltpu.make_async_copy(source, target, sem.at[len(copies)])
        copy.start()
        copies.append(copy)

    send(features_ref, features_hbm)
    for h in range(2):
        lanes = slice(h * H, (h + 1) * H)
        zero_ref[:, lanes] = small_ref[h, :10, :]
        gain_ref[:, lanes] = small_ref[h, 10:11, :]
        bias_ref[:, lanes] = small_ref[h, 11:12, :]
    send(zero_ref, zero_hbm)
    send(gain_ref, gain_hbm)
    send(bias_ref, bias_hbm)
    chunk = per // 4
    for i in range(8):
        at = slice(i * chunk, (i + 1) * chunk)
        for h in range(2):
            wide_ref[at, h * H : (h + 1) * H] = res_ref[h, at, :].astype(F32)
        target = two_hbm if i < 4 else one_hbm
        begin = (i % 4) * chunk
        send(wide_ref.at[at, :], target.at[begin : begin + chunk, :])
    for copy in copies:
        copy.wait()


def shards(tm, rec, audio, conv0_weight, norm_gain, norm_bias, conv1_weight, conv2_weight, cotangent):
    samples = audio.shape[1]
    rows = samples // 20
    rows_all = rows + EDGE
    C = conv0_weight.shape[1]
    H = C // 2
    total_rows = 6 * C
    part_rows = total_rows // PARTS
    plans = plan(tm, rec, part_rows)
    received = max(recv_rows(stages, part_rows) for stages in plans)
    most = max(members for stages in plans for _, _, members, _, _ in stages)
    stages = len(plans[0])
    chips = tm // 2
    vmem = pl.BlockSpec(memory_space=pltpu.VMEM)
    hbm = pl.BlockSpec(memory_space=pltpu.HBM)
    dma = pltpu.SemaphoreType.DMA
    features, res, small = pl.pallas_call(
        functools.partial(kernel, tm, rec),
        out_shape=(
            jax.ShapeDtypeStruct((rows, C), BF16),
            jax.ShapeDtypeStruct((2, total_rows, H), BF16),
            jax.ShapeDtypeStruct((2, 16, H), F32),
        ),
        in_specs=[hbm] * 7,
        out_specs=(vmem,) * 3,
        scratch_shapes=[
            pltpu.VMEM((samples // 128, 128), F32),
            pltpu.VMEM((10, C), F32),
            pltpu.VMEM((1, C), F32),
            pltpu.VMEM((1, C), F32),
            pltpu.VMEM((rows_all, C), BF16),
            pltpu.VMEM((128, 128), F32),
            pltpu.VMEM((rows_all, 256), BF16),
            pltpu.VMEM((256, 4 * C), BF16),
            pltpu.VMEM((INFO, 128), F32),
            pltpu.VMEM((tm, INFO, 128), F32),
            pltpu.VMEM((rows_all, 4 * C), F32),
            pltpu.VMEM((rows_all, 5 * C), BF16),
            pltpu.VMEM((rows_all, 2 * C), F32),
            pltpu.VMEM((rows_all, 3 * C), BF16),
            pltpu.VMEM((rows_all, C), BF16),
            pltpu.VMEM((rows_all, 2 * C), BF16),
            pltpu.VMEM((rows_all, 128), F32),
            pltpu.VMEM((rows, 4 * C), F32),
            pltpu.VMEM((rows_all, 3 * C), F32),
            pltpu.VMEM((rows_all, 3 * C), F32),
            pltpu.VMEM((PARTS, part_rows, H), F32),
            pltpu.VMEM((PARTS, part_rows, H), BF16),
            pltpu.VMEM((PARTS, part_rows, H), BF16),
            pltpu.VMEM((PARTS, received, H), BF16),
            pltpu.VMEM((2, 16, H), F32),
            pltpu.VMEM((16, H), F32),
            pltpu.VMEM((chips, 16, H), F32),
            pltpu.VMEM((rec, 16, H), F32),
            pltpu.VMEM((3 * C, C), BF16),
            pltpu.VMEM((3 * C, C), BF16),
            dma((7,)),
            dma,
            dma,
            dma((tm,)),
            dma((tm,)),
            dma((PARTS, 2)),
            dma((PARTS, 2)),
            dma((PARTS, stages, most)),
            dma((PARTS, stages, most)),
            dma((PARTS, stages, most)),
            dma((PARTS, stages, most)),
            dma((chips + rec + 1,)),
            dma((chips + rec + 1,)),
        ],
        compiler_params=pltpu.CompilerParams(
            collective_id=0, has_side_effects=True, vmem_limit_bytes=44 * 2**20
        ),
    )(*(
        pltpu.with_memory_space_constraint(value, pltpu.HBM)
        for value in (
            audio.reshape(samples // 128, 128), conv0_weight, norm_gain[None, :], norm_bias[None, :],
            conv1_weight, conv2_weight, cotangent[0],
        )
    ))
    features, grad_zero, grad_gain, grad_bias, grad_one, grad_two = pl.pallas_call(
        finish,
        out_shape=(
            jax.ShapeDtypeStruct((rows, C), BF16),
            jax.ShapeDtypeStruct((10, C), F32),
            jax.ShapeDtypeStruct((1, C), F32),
            jax.ShapeDtypeStruct((1, C), F32),
            jax.ShapeDtypeStruct((3 * C, C), F32),
            jax.ShapeDtypeStruct((3 * C, C), F32),
        ),
        in_specs=[vmem] * 3,
        out_specs=(hbm,) * 6,
        scratch_shapes=[
            pltpu.VMEM((total_rows, C), F32),
            pltpu.VMEM((10, C), F32),
            pltpu.VMEM((1, C), F32),
            pltpu.VMEM((1, C), F32),
            dma((12,)),
        ],
        compiler_params=pltpu.CompilerParams(vmem_limit_bytes=24 * 2**20),
    )(features, res, small)
    return (features[None], grad_zero, grad_gain[0], grad_bias[0], grad_one, grad_two)


def solution(mesh):
    return jax.shard_map(
        functools.partial(shards, mesh.shape["tm"], mesh.shape["rec"]),
        mesh=mesh,
        in_specs=(P("rec", "tm"), P(), P(), P(), P(), P(), P("rec", "tm", None)),
        out_specs=(P("rec", "tm", None), P(), P(), P(), P(), P()),
        check_vma=False,
    )
```

```python
import functools

import jax
import jax.numpy as jnp
from jax import lax
from jax.experimental import pallas as pl
from jax.experimental.pallas import tpu as pltpu
from jax.sharding import PartitionSpec as P

EPS = 1e-05
HIGH = lax.Precision.HIGHEST
MESH = pl.DeviceIdType.MESH
F32, BF16 = jnp.float32, jnp.bfloat16
EDGE = 16
STEP = 16
PARTS = 6
PLANS = {2: 'zp'}
ORDER = (
    1, 2, 6, 1, 2, 4, 0, 0, 6, 4, 6, 1, 6, 6, 5, 3, 6, 6, 6, 5, 0, 2, 6, 1,
    3, 6, 4, 6, 6, 0, 6, 5, 1, 4, 3, 2, 0, 5, 6, 4, 1, 3, 2, 5, 0, 6, 4, 3,
    5, 2, 3,
)
INFO = 24


def gelu_parts(value):
    phi = 0.5 * (1.0 + lax.erf(value * 0.7071067811865476))
    slope = phi + value * jnp.exp(-0.5 * value * value) * 0.3989422804014327
    return value * phi, slope


def dot(a, b, ca, cb, precision=None):
    return lax.dot_general(
        a, b, (((ca,), (cb,)), ((), ())), precision=precision, preferred_element_type=F32
    )


def axes_of(tm, rec):
    plane = [1 << i for i in range(1, tm.bit_length() - 1)]
    return {"p": ("tm", plane), "z": ("rec", [1 << i for i in range(rec.bit_length() - 1)])}


def plan(tm, rec, rows):
    axes, plans = axes_of(tm, rec), []
    for part in range(PARTS):
        size, stages = rows, []
        for name in PLANS.get(part, "pz"):
            axis, bits = axes[name]
            members = 1 << len(bits)
            whole = size // members < 16 or size % (16 * members) != 0
            size = size if whole else size // members
            stages.append((axis, bits, members, size, whole))
        plans.append(stages)
    return plans


def recv_rows(stages, rows):
    return rows + sum(size * members for _, _, members, size, _ in stages)


def kernel(
    tm, rec, audio_hbm, taps_hbm, gain_hbm, bias_hbm, w1_hbm, w2_hbm, cot_hbm,
    features_ref, res_ref, small_ref,
    audio_ref, taps_ref, gain_ref, bias_ref, cot_ref, gram_ref, lhs_ref, wide_ref, info_ref, info_in,
    norm_ref, act0_ref, slope1_ref, act1_ref, delta2_ref, delta1_ref,
    xx_ref, dn_ref, t0_ref, t1_ref, gf_ref, corebuf, sendbuf, recvbuf, lit_ref, lit_core, lit_xy, lit_z,
    w1_ref, w2_ref, load_sem, ed_send, ed_recv, in_send, in_recv, co_send, co_recv, rs_send, rs_recv, ag_send, ag_recv,
    sm_send, sm_recv,
):
    me = {"tm": lax.axis_index("tm"), "rec": lax.axis_index("rec")}
    rows_all, C = delta2_ref.shape
    H = C // 2
    rows = rows_all - EDGE
    count = 4.0 * rows * tm
    inside = 4.0 * rows - 1.0
    part_rows = gf_ref.shape[1]
    plans = plan(tm, rec, part_rows)
    core = lax.rem(me["tm"], 2)
    sibling = {"tm": me["tm"] + 1 - 2 * core}

    def bit_of(axis, bit):
        return lax.rem(me[axis] // bit, 2)

    def place(axis, bits, mask=0):
        where = 0
        for i, bit in enumerate(bits):
            own = bit_of(axis, bit)
            where = where + ((1 - own) if mask >> i & 1 else own) * (1 << i)
        return where

    def partner(axis, bits, mask):
        index = me[axis]
        for i, bit in enumerate(bits):
            if mask >> i & 1:
                index = index + bit * (1 - 2 * bit_of(axis, bit))
        return {axis: index}

    loads = [
        pltpu.make_async_copy(source, target, load_sem.at[i])
        for i, (source, target) in enumerate((
            (audio_hbm, audio_ref), (taps_hbm, taps_ref), (gain_hbm, gain_ref), (bias_hbm, bias_ref),
            (cot_hbm, cot_ref.at[:rows, :]), (w1_hbm, w1_ref), (w2_hbm, w2_ref),
        ))
    ]
    loads[0].start()
    barrier = pltpu.get_barrier_semaphore()
    for d in range(1, tm):
        pl.semaphore_signal(barrier, inc=1, device_id={"tm": lax.rem(me["tm"] + d, tm)}, device_id_type=MESH)
    for d in range(1, rec):
        pl.semaphore_signal(barrier, inc=1, device_id={"rec": lax.rem(me["rec"] + d, rec)}, device_id_type=MESH)

    for load in loads[1:]:
        load.start()

    loads[0].wait()
    groups = rows // 32
    blocks = [audio_ref[pl.ds(k, groups, stride=5), :] for k in range(5)]
    blocks.append(pltpu.roll(blocks[0], groups - 1, 0))
    lane = lax.broadcasted_iota(jnp.int32, (groups, 128), 1)
    for s in range(32):
        k, off = divmod(20 * s, 128)
        piece = blocks[k]
        if off:
            piece = pltpu.roll(piece, 128 - off, 1)
        if off + 25 > 128:
            piece = jnp.where(lane < 128 - off, piece, pltpu.roll(blocks[k + 1], 128 - off, 1))
        xx_ref[pl.ds(s, groups, stride=32), :] = jnp.where(lane < 25, piece, 0.0)
    shift = jnp.sum(jnp.sum(audio_ref[...], 0, keepdims=True), 1, keepdims=True) / (20.0 * rows)
    x = xx_ref[:rows, :]
    lane = lax.broadcasted_iota(jnp.int32, x.shape, 1)
    row = lax.broadcasted_iota(jnp.int32, x.shape, 0)
    level = x - shift
    last = jnp.logical_and(jnp.logical_and(lane >= 32, lane < 42), row < rows - 1)
    level = jnp.where(lane < 20, level, jnp.where(last, pltpu.roll(level, 17, 1), jnp.where(lane == 64, 1.0, 0.0)))
    gram_ref[...] = dot(level, level, 0, 0, HIGH)
    lane16 = lax.broadcasted_iota(jnp.int32, (16, 128), 1)
    gram, column, line = 0.0, 0.0, 0.0
    ones_row = gram_ref[64:65, :]
    for k in (0, 5, 10, 32):
        piece = gram_ref[k : k + 16, :]
        column = column + piece[:, 64:65]
        gram = gram + (pltpu.roll(piece, 128 - k, 1) if k else piece)
        line = line + (pltpu.roll(ones_row, 128 - k, 1) if k else ones_row)
    info_ref[:16, :] = jnp.where(lane16 < 10, gram, jnp.where(lane16 == 10, column, 0.0))
    info_ref[16:17, :] = line
    info_ref[17:18, :] = xx_ref[0:1, :]
    info_ref[18:19, :] = xx_ref[rows - 1 : rows, :]
    info_ref[19:20, :] = jnp.broadcast_to(shift, (1, 128))
    info_ref[20:, :] = jnp.zeros((INFO - 20, 128), F32)
    info_in[0] = info_ref[...]
    pl.semaphore_wait(barrier, tm - 1 + rec - 1)
    infos = []
    for d in range(1, tm):
        copy = pltpu.make_async_remote_copy(
            src_ref=info_ref, dst_ref=info_in.at[d], send_sem=in_send.at[d], recv_sem=in_recv.at[d],
            device_id={"tm": lax.rem(me["tm"] + d, tm)}, device_id_type=MESH,
        )
        copy.start()
        infos.append(copy)
    loads[4].wait()
    edge_copy = pltpu.make_async_remote_copy(
        src_ref=cot_ref.at[rows - 16 : rows, :], dst_ref=cot_ref.at[rows:, :], send_sem=ed_send, recv_sem=ed_recv,
        device_id={"tm": lax.rem(me["tm"] + 1, tm)}, device_id_type=MESH,
    )
    edge_copy.start()

    loads[1].wait()
    loads[2].wait()
    loads[3].wait()
    taps = taps_ref[...]
    padded = jnp.concatenate([taps, jnp.zeros((22, C), F32)], 0)
    for q in range(4):
        lanes = slice(q * C, (q + 1) * C)
        value = pltpu.roll(padded, 5 * q, 0) if q else padded
        one = value.astype(BF16)
        rest = value - one.astype(F32)
        two = rest.astype(BF16)
        three = (rest - two.astype(F32)).astype(BF16)
        for i, term in enumerate((one, two, one, two, three, one)):
            wide_ref[32 * i : 32 * (i + 1), lanes] = term
        wide_ref[192:, lanes] = jnp.zeros((64, C), BF16)

    def first_conv(begin, end):
        value = xx_ref[begin:end, :]
        one = value.astype(BF16).astype(F32)
        rest = value - one
        two = rest.astype(BF16).astype(F32)
        three = rest - two
        lhs_ref[begin:end, :128] = (
            one + pltpu.roll(one, 32, 1) + pltpu.roll(two, 64, 1) + pltpu.roll(two, 96, 1)
        ).astype(BF16)
        lhs_ref[begin:end, 128:] = (one + pltpu.roll(three, 32, 1)).astype(BF16)
        norm_ref[begin:end, :] = dot(lhs_ref[begin:end, :], wide_ref[...], 1, 0)

    first_conv(0, rows - 16)
    for copy in infos:
        copy.wait_recv()

    center = info_in[0, 19:20, :]
    for d in range(1, tm):
        center = center + info_in[d, 19:20, :]
    center = center / tm
    gram, column, line = 0.0, 0.0, 0.0
    for d in range(tm):
        off = info_in[d, 19:20, :] - center
        piece, own_line = info_in[d, :16, :], info_in[d, 16:17, :]
        own_column = piece[:, 10:11]
        gram = gram + piece + off * (own_column + own_line + inside * off)
        column = column + own_column + inside * off[:, :1]
        line = line + own_line + inside * off
    ends, starts = info_in[:, 18, :], info_in[:, 17, :]
    lane = lax.broadcasted_iota(jnp.int32, ends.shape, 1)
    slot = lax.broadcasted_iota(jnp.int32, ends.shape, 0)
    starts = jnp.where(slot == lax.rem(me["tm"] + 1, tm), 0.0, pltpu.roll(pltpu.roll(starts, 5, 1), 1, 0))
    cross = jnp.where(lane < 5, pltpu.roll(ends, 113, 1), starts) - center
    cross = jnp.where(lane < 10, cross, jnp.where(lane == 10, 1.0, 0.0))
    extra = dot(cross, cross, 0, 0, HIGH)
    gram = gram + extra[:16, :]
    column = (column + extra[:16, 10:11]) / count
    line = (line + extra[10:11, :]) / count
    spread = gram / count - column * line
    taps16 = padded[:16, :]
    through = spread[:, 0:1] * taps[0:1, :]
    for j in range(1, 10):
        through = through + spread[:, j : j + 1] * taps[j : j + 1, :]
    variance = jnp.maximum(jnp.sum(taps16 * through, 0, keepdims=True), 0.0)
    mean = jnp.sum(taps16 * (column + center[:, :1]), 0, keepdims=True)
    inverse = lax.rsqrt(variance + EPS)
    gain, bias = gain_ref[...], bias_ref[...]

    lane = lax.broadcasted_iota(jnp.int32, (16, 128), 1)
    row = lax.broadcasted_iota(jnp.int32, (16, 128), 0)
    after = jnp.where(me["tm"] == tm - 1, 0.0, info_in[tm - 1, 17:18, :])
    before = jnp.where(me["tm"] == 0, 0.0, info_in[1, 18:19, :])
    before = jnp.where(lane[:1] < 20, before, pltpu.roll(info_ref[17:18, :], 20, 1))
    tail = xx_ref[rows - 16 : rows, :]
    fill = jnp.logical_and(row == 15, jnp.logical_and(lane >= 20, lane < 25))
    xx_ref[rows - 16 : rows, :] = jnp.where(fill, pltpu.roll(after, 20, 1), tail)
    xx_ref[rows:, :] = jnp.where(
        lane < 25, jnp.where(row == 0, after, jnp.where(row == 15, before, 0.0)), 0.0
    )
    first_conv(rows - 16, rows_all)

    scale = gain * inverse

    def first_act(at, q):
        lanes = slice(q * C, (q + 1) * C)
        shifted = (norm_ref[at, lanes] - mean) * scale + bias
        act0_ref[at, lanes] = (shifted * (0.5 * (1.0 + lax.erf(shifted * 0.7071067811865476)))).astype(BF16)

    def first_rows(i, carry):
        for q in range(4):
            first_act(pl.ds(pl.multiple_of(i * STEP, STEP), STEP), q)
        return carry

    lax.fori_loop(0, rows_all // STEP, first_rows, 0, unroll=True)

    @pl.when(me["tm"] == tm - 1)
    def _():
        row = lax.broadcasted_iota(jnp.int32, (EDGE, 4 * C), 0)
        act0_ref[rows:, : 4 * C] = jnp.where(row == 0, 0.0, act0_ref[rows:, : 4 * C].astype(F32)).astype(BF16)

    act0_ref[:, 4 * C :] = pltpu.roll(act0_ref[:, :C].astype(F32), rows_all - 1, 0).astype(BF16)

    loads[5].wait()

    def second_act(half, block):
        lanes = slice(half * C + block * H, half * C + (block + 1) * H)
        value = dot(act0_ref[:, 2 * half * C : (2 * half + 3) * C], w1_ref[:, block * H : (block + 1) * H], 1, 0)
        act, slope = gelu_parts(value)
        act1_ref[:, lanes] = act.astype(BF16)
        slope1_ref[:, lanes] = slope

    second_act(0, 0)
    second_act(0, 1)
    second_act(1, 0)
    second_act(1, 1)

    @pl.when(me["tm"] == tm - 1)
    def _():
        row = lax.broadcasted_iota(jnp.int32, (EDGE, 2 * C), 0)
        act1_ref[rows:, : 2 * C] = jnp.where(row == 0, 0.0, act1_ref[rows:, : 2 * C].astype(F32)).astype(BF16)

    act1_ref[:, 2 * C :] = pltpu.roll(act1_ref[:, :C].astype(F32), rows_all - 1, 0).astype(BF16)

    loads[6].wait()
    edge_copy.wait_recv()

    @pl.when(me["tm"] == 0)
    def _():
        cot_ref[rows:, :] = jnp.zeros((EDGE, C), BF16)

    mine = pl.ds(pl.multiple_of(core * H, H), H)
    other = pl.ds(pl.multiple_of((1 - core) * H, H), H)

    def third_act(lanes, value):
        act, slope = gelu_parts(value)
        features_ref[:, lanes] = act[:rows].astype(BF16)
        delta2_ref[:, lanes] = (cot_ref[:, lanes].astype(F32) * slope).astype(BF16)

    theirs = dot(act1_ref[...], w2_ref[:, other], 1, 0)
    own = dot(act1_ref[...], w2_ref[:, mine], 1, 0)
    third_act(other, theirs)

    state = [
        {"size": part_rows, "start": 0, "used": part_rows, "step": 0, "wait": [], "sent": [], "bases": [0], "kept": []}
        for _ in range(PARTS)
    ]

    def combine(target, offset, part, start, size, began, bases):
        block = min(32, size)

        def body(i, carry):
            at = pl.ds(pl.multiple_of(start + i * block, 16), block)
            value = gf_ref[part, at, :]
            for base in bases:
                came = pl.ds(pl.multiple_of(base + (start - began) + i * block, 16), block)
                value = value + recvbuf[part, came, :].astype(F32)
            to = pl.ds(pl.multiple_of(offset + start + i * block, 16), block)
            target[to, :] = value.astype(target.dtype)
            return carry

        lax.fori_loop(0, size // block, body, 0)

    def settle(part, start, size, base, members):
        block = min(32, size)

        def body(i, carry):
            value = 0.0
            for slot in range(members):
                came = pl.ds(pl.multiple_of(base + slot * size + i * block, 16), block)
                value = value + recvbuf[part, came, :].astype(F32)
            gf_ref[part, pl.ds(pl.multiple_of(start + i * block, 16), block), :] = value
            return carry

        lax.fori_loop(0, size // block, body, 0)

    def start_core(part, value):
        corebuf[part] = value.astype(BF16)
        copy = pltpu.make_async_remote_copy(
            src_ref=corebuf.at[part], dst_ref=recvbuf.at[part, pl.ds(0, part_rows), :],
            send_sem=co_send.at[part, 0], recv_sem=co_recv.at[part, 0], device_id=sibling, device_id_type=MESH,
        )
        copy.start()
        state[part]["wait"] = [copy]
        state[part]["sent"].append(copy)

    def advance(part):
        s, stages = state[part], plans[part]
        step = s["step"]
        s["step"] += 1
        for copy in s["wait"]:
            copy.wait_recv()
        s["wait"] = []
        size, start = s["size"], s["start"]
        if step <= len(stages) and step > 0 and stages[step - 1][4]:
            settle(part, start, size, s["bases"][0], stages[step - 1][2])
            s["bases"] = []
        if step < len(stages):
            axis, bits, members, out, whole = stages[step]
            here = place(axis, bits)
            base = s["used"]
            for mask in range(members - 1, 0, -1):
                there = place(axis, bits, mask)
                if whole:
                    away = start
                    if mask == members - 1:
                        combine(sendbuf.at[part], 0, part, start, size, start, s["bases"])
                        own = pl.ds(pl.multiple_of(base + here * size, 16), size)
                        recvbuf[part, own, :] = sendbuf[part, pl.ds(pl.multiple_of(start, 16), size), :]
                    to = base + here * size
                else:
                    away = start + there * out
                    combine(sendbuf.at[part], 0, part, away, out, start, s["bases"])
                    to = base + (mask - 1) * out
                copy = pltpu.make_async_remote_copy(
                    src_ref=sendbuf.at[part, pl.ds(pl.multiple_of(away, 16), out), :],
                    dst_ref=recvbuf.at[part, pl.ds(pl.multiple_of(to, 16), out), :],
                    send_sem=rs_send.at[part, step, mask], recv_sem=rs_recv.at[part, step, mask],
                    device_id=partner(axis, bits, mask), device_id_type=MESH,
                )
                copy.start()
                s["wait"].append(copy)
                s["sent"].append(copy)
            if whole:
                s["bases"] = [base]
                s["kept"].append(None)
            else:
                keep = start + here * out
                combine(gf_ref.at[part], 0, part, keep, out, start, s["bases"])
                s["bases"] = [base + i * out for i in range(members - 1)]
                s["kept"].append((keep, out))
                s["start"] = keep
            s["size"], s["used"] = out, base + members * out
            return
        if step == len(stages):
            combine(res_ref.at[core], part * part_rows, part, start, size, start, s["bases"])
        back = 2 * len(stages) - 1 - step
        while back >= 0 and s["kept"][back] is None:
            back -= 1
            s["step"] += 1
        if back >= 0:
            axis, bits, members, _, _ = stages[back]
            keep, out = s["kept"][back]
            piece = res_ref.at[core, pl.ds(pl.multiple_of(part * part_rows + keep, 16), out), :]
            for mask in range(members - 1, 0, -1):
                copy = pltpu.make_async_remote_copy(
                    src_ref=piece, dst_ref=piece,
                    send_sem=ag_send.at[part, back, mask], recv_sem=ag_recv.at[part, back, mask],
                    device_id=partner(axis, bits, mask), device_id_type=MESH,
                )
                copy.start()
                s["wait"].append(copy)
                s["sent"].append(copy)
        elif back == -1:
            piece = res_ref.at[core, pl.ds(part * part_rows, part_rows), :]
            copy = pltpu.make_async_remote_copy(
                src_ref=piece, dst_ref=piece, send_sem=co_send.at[part, 1], recv_sem=co_recv.at[part, 1],
                device_id=sibling, device_id_type=MESH,
            )
            copy.start()
            s["wait"].append(copy)
            s["sent"].append(copy)

    half = PARTS // 2

    def weight_grad(part, lanes):
        begin = (part % half) * part_rows
        one = slice(begin, begin + part_rows)
        two = slice(2 * C + begin, 2 * C + begin + part_rows)
        if part < half:
            return dot(act1_ref[:rows, one], delta2_ref[:rows, lanes], 0, 0)
        first, second = delta1_ref.at[:rows, :C], delta1_ref.at[:rows, C:]
        return dot(act0_ref[:rows, one], first[:, lanes], 0, 0) + dot(act0_ref[:rows, two], second[:, lanes], 0, 0)

    def advance_part(part):
        step = state[part]["step"]
        if step == 0 and not state[part]["sent"]:
            start_core(part, weight_grad(part, other))
            return
        if step == 0:
            gf_ref[part] = weight_grad(part, mine)
        if step <= 2 * len(plans[part]) + 2:
            advance(part)

    def second_delta():
        t0_ref[...] = dot(delta2_ref[...], w2_ref[...], 1, 1)
        even = t0_ref[:, :C] + pltpu.roll(t0_ref[:, 2 * C :], 1, 0)
        delta1_ref[:, :C] = (even * slope1_ref[:, :C]).astype(BF16)
        delta1_ref[:, C:] = (t0_ref[:, C : 2 * C] * slope1_ref[:, C:]).astype(BF16)

    def even_back():
        t0_ref[...] = dot(delta1_ref[:, :C], w1_ref[...], 1, 1)

    def odd_back():
        t1_ref[...] = dot(delta1_ref[:, C:], w1_ref[...], 1, 1)
        t1_ref[:, 2 * C :] = pltpu.roll(t1_ref[:, 2 * C :], 1, 0)

    zero = jnp.zeros((STEP, C), F32)

    def back(i, carry):
        one, two = carry
        at = pl.ds(pl.multiple_of(i * STEP, STEP), STEP)
        grads = (
            t0_ref[at, :C] + t1_ref[at, 2 * C :],
            t0_ref[at, C : 2 * C],
            t0_ref[at, 2 * C :] + t1_ref[at, :C],
            t1_ref[at, C : 2 * C],
        )
        for q in range(4):
            lanes = slice(q * C, (q + 1) * C)
            normed = (norm_ref[at, lanes] - mean) * inverse
            dnorm = grads[q] * gelu_parts(normed * gain + bias)[1]
            dn_ref[at, lanes] = dnorm
            one = one + dnorm
            two = two + dnorm * normed
        return one, two

    sums = {"both": (zero, zero), "taps": jnp.zeros((32, C), F32)}
    quarter = rows // STEP // 4

    def back_rows(i):
        sums["both"] = lax.fori_loop(i * quarter, (i + 1) * quarter, back, sums["both"])

    def taps_of(q):
        samples = xx_ref[:rows, :] - center
        total = dot(samples[:, :32], dn_ref[:, q * C : (q + 1) * C], 0, 0, HIGH)
        sums["taps"] = sums["taps"] + (pltpu.roll(total, 32 - 5 * q, 0) if q else total)

    def small_grads():
        local_one, local_two = (jnp.sum(value, 0, keepdims=True) for value in sums["both"])
        grad_zero = scale * (sums["taps"][:16] - local_one * column - (local_two * inverse) * through)
        row = lax.broadcasted_iota(jnp.int32, (16, C), 0)
        little = jnp.where(row < 10, grad_zero, jnp.where(row == 10, local_two, jnp.where(row == 11, local_one, 0.0)))
        lit_ref[0], lit_ref[1] = little[:, :H], little[:, H:]

    plane, z = (axes_of(tm, rec)[name] for name in "pz")
    small_state = {"wait": [], "sent": [], "step": 0}

    def send_small(source, target, group, device):
        copy = pltpu.make_async_remote_copy(
            src_ref=source, dst_ref=target, send_sem=sm_send.at[group], recv_sem=sm_recv.at[group],
            device_id=device, device_id_type=MESH,
        )
        copy.start()
        small_state["wait"].append(copy)
        small_state["sent"].append(copy)

    def spread_small(buffer, axis, bits, first_sem):
        here = buffer.at[place(axis, bits)]
        for mask in range(1, 1 << len(bits)):
            send_small(here, here, first_sem + mask, partner(axis, bits, mask))

    def total_of(buffer):
        total = buffer[0]
        for i in range(1, buffer.shape[0]):
            total = total + buffer[i]
        return total

    def advance_small():
        step = small_state["step"]
        small_state["step"] += 1
        for copy in small_state["wait"]:
            copy.wait_recv()
        small_state["wait"] = []
        if step == 0:
            send_small(lit_ref.at[1 - core], lit_core, 0, sibling)
        elif step == 1:
            lit_xy[place(*plane)] = lit_ref[core] + lit_core[...]
            spread_small(lit_xy, *plane, 0)
        elif step == 2:
            lit_z[place(*z)] = total_of(lit_xy)
            spread_small(lit_z, *z, lit_xy.shape[0])
        elif step == 3:
            small_ref[core] = total_of(lit_z)
            send_small(small_ref.at[core], small_ref.at[core], lit_xy.shape[0] + lit_z.shape[0], sibling)

    def first_small():
        small_grads()
        advance_small()

    main = [second_delta, even_back, odd_back]
    main += [functools.partial(back_rows, i) for i in range(4)] + [functools.partial(taps_of, q) for q in range(4)]
    main += [first_small] + [advance_small] * 4
    early = next(i for i, item in enumerate(ORDER) if item >= half or item in ORDER[:i])
    for item in ORDER[:early]:
        advance_part(item)
    third_act(mine, own)
    for item in ORDER[early:]:
        if item < PARTS:
            advance_part(item)
        elif main:
            main.pop(0)()
    for work in main:
        work()
    while min(s["step"] - 2 * len(p) for s, p in zip(state, plans)) < 3:
        for part in range(PARTS):
            advance_part(part)
    for s in state:
        for copy in s["sent"]:
            copy.wait_send()
    for copy in small_state["sent"] + infos + [edge_copy]:
        copy.wait_send()


def finish(
    features_ref, res_ref, small_ref, features_hbm, zero_hbm, gain_hbm, bias_hbm, one_hbm, two_hbm,
    wide_ref, zero_ref, gain_ref, bias_ref, sem,
):
    H = res_ref.shape[2]
    per = one_hbm.shape[0]
    copies = []

    def send(source, target):
        copy = pltpu.make_async_copy(source, target, sem.at[len(copies)])
        copy.start()
        copies.append(copy)

    send(features_ref, features_hbm)
    for h in range(2):
        lanes = slice(h * H, (h + 1) * H)
        zero_ref[:, lanes] = small_ref[h, :10, :]
        gain_ref[:, lanes] = small_ref[h, 10:11, :]
        bias_ref[:, lanes] = small_ref[h, 11:12, :]
    send(zero_ref, zero_hbm)
    send(gain_ref, gain_hbm)
    send(bias_ref, bias_hbm)
    chunk = per // 4
    for i in range(8):
        at = slice(i * chunk, (i + 1) * chunk)
        for h in range(2):
            wide_ref[at, h * H : (h + 1) * H] = res_ref[h, at, :].astype(F32)
        target = two_hbm if i < 4 else one_hbm
        begin = (i % 4) * chunk
        send(wide_ref.at[at, :], target.at[begin : begin + chunk, :])
    for copy in copies:
        copy.wait()


def shards(tm, rec, audio, conv0_weight, norm_gain, norm_bias, conv1_weight, conv2_weight, cotangent):
    samples = audio.shape[1]
    rows = samples // 20
    rows_all = rows + EDGE
    C = conv0_weight.shape[1]
    H = C // 2
    total_rows = 6 * C
    part_rows = total_rows // PARTS
    plans = plan(tm, rec, part_rows)
    received = max(recv_rows(stages, part_rows) for stages in plans)
    most = max(members for stages in plans for _, _, members, _, _ in stages)
    stages = len(plans[0])
    chips = tm // 2
    vmem = pl.BlockSpec(memory_space=pltpu.VMEM)
    hbm = pl.BlockSpec(memory_space=pltpu.HBM)
    dma = pltpu.SemaphoreType.DMA
    features, res, small = pl.pallas_call(
        functools.partial(kernel, tm, rec),
        out_shape=(
            jax.ShapeDtypeStruct((rows, C), BF16),
            jax.ShapeDtypeStruct((2, total_rows, H), BF16),
            jax.ShapeDtypeStruct((2, 16, H), F32),
        ),
        in_specs=[hbm] * 7,
        out_specs=(vmem,) * 3,
        scratch_shapes=[
            pltpu.VMEM((samples // 128, 128), F32),
            pltpu.VMEM((10, C), F32),
            pltpu.VMEM((1, C), F32),
            pltpu.VMEM((1, C), F32),
            pltpu.VMEM((rows_all, C), BF16),
            pltpu.VMEM((128, 128), F32),
            pltpu.VMEM((rows_all, 256), BF16),
            pltpu.VMEM((256, 4 * C), BF16),
            pltpu.VMEM((INFO, 128), F32),
            pltpu.VMEM((tm, INFO, 128), F32),
            pltpu.VMEM((rows_all, 4 * C), F32),
            pltpu.VMEM((rows_all, 5 * C), BF16),
            pltpu.VMEM((rows_all, 2 * C), F32),
            pltpu.VMEM((rows_all, 3 * C), BF16),
            pltpu.VMEM((rows_all, C), BF16),
            pltpu.VMEM((rows_all, 2 * C), BF16),
            pltpu.VMEM((rows_all, 128), F32),
            pltpu.VMEM((rows, 4 * C), F32),
            pltpu.VMEM((rows_all, 3 * C), F32),
            pltpu.VMEM((rows_all, 3 * C), F32),
            pltpu.VMEM((PARTS, part_rows, H), F32),
            pltpu.VMEM((PARTS, part_rows, H), BF16),
            pltpu.VMEM((PARTS, part_rows, H), BF16),
            pltpu.VMEM((PARTS, received, H), BF16),
            pltpu.VMEM((2, 16, H), F32),
            pltpu.VMEM((16, H), F32),
            pltpu.VMEM((chips, 16, H), F32),
            pltpu.VMEM((rec, 16, H), F32),
            pltpu.VMEM((3 * C, C), BF16),
            pltpu.VMEM((3 * C, C), BF16),
            dma((7,)),
            dma,
            dma,
            dma((tm,)),
            dma((tm,)),
            dma((PARTS, 2)),
            dma((PARTS, 2)),
            dma((PARTS, stages, most)),
            dma((PARTS, stages, most)),
            dma((PARTS, stages, most)),
            dma((PARTS, stages, most)),
            dma((chips + rec + 1,)),
            dma((chips + rec + 1,)),
        ],
        compiler_params=pltpu.CompilerParams(
            collective_id=0, has_side_effects=True, vmem_limit_bytes=44 * 2**20
        ),
    )(*(
        pltpu.with_memory_space_constraint(value, pltpu.HBM)
        for value in (
            audio.reshape(samples // 128, 128), conv0_weight, norm_gain[None, :], norm_bias[None, :],
            conv1_weight, conv2_weight, cotangent[0],
        )
    ))
    features, grad_zero, grad_gain, grad_bias, grad_one, grad_two = pl.pallas_call(
        finish,
        out_shape=(
            jax.ShapeDtypeStruct((rows, C), BF16),
            jax.ShapeDtypeStruct((10, C), F32),
            jax.ShapeDtypeStruct((1, C), F32),
            jax.ShapeDtypeStruct((1, C), F32),
            jax.ShapeDtypeStruct((3 * C, C), F32),
            jax.ShapeDtypeStruct((3 * C, C), F32),
        ),
        in_specs=[vmem] * 3,
        out_specs=(hbm,) * 6,
        scratch_shapes=[
            pltpu.VMEM((total_rows, C), F32),
            pltpu.VMEM((10, C), F32),
            pltpu.VMEM((1, C), F32),
            pltpu.VMEM((1, C), F32),
            dma((12,)),
        ],
        compiler_params=pltpu.CompilerParams(vmem_limit_bytes=24 * 2**20),
    )(features, res, small)
    return (features[None], grad_zero, grad_gain[0], grad_bias[0], grad_one, grad_two)


def solution(mesh):
    return jax.shard_map(
        functools.partial(shards, mesh.shape["tm"], mesh.shape["rec"]),
        mesh=mesh,
        in_specs=(P("rec", "tm"), P(), P(), P(), P(), P(), P("rec", "tm", None)),
        out_specs=(P("rec", "tm", None), P(), P(), P(), P(), P()),
        check_vma=False,
    )
```
